128 devices in a mesh: grp: 64 (over z, y, x), dom: 2 (over core).
Axes of the slice: x: 4, y: 4, z: 4, core: 2. Of those that a mesh axis runs over, the one named last changes fastest.
Arguments:
- residual: float32 [64, 2048], P('grp', 'dom'), may hold values from -6 to 6
- op_blocks: float32 [64, 32, 64, 1728], P('grp', 'dom'), may hold values from -1 to 4
- block_cols: int32 [64, 32, 27], P('grp', 'dom'), may hold values from 0 to 47, as said below
- restrict_one: float32 [64, 64, 2048], P('grp', None, 'dom'), may hold values from -1 to 1
- restrict_two: float32 [64, 1024], P(None, 'dom'), may hold values from -1 to 1
- agg_one: int32 [16], replicated, may hold values from 0 to 15, each once
- agg_two: int32 [8], replicated, may hold values from 0 to 7, each once
Outputs:
- correction: float32 [64, 2048], P('grp', 'dom')
The draws below stay inside these ranges and needn't reach their ends.
Inputs may be any that keep to these rules, and one draw needn't show every extreme that they name: `block_cols`: entry 0 of every row is the row's own block, 16 + (row index mod 16); an entry c names a block of the previous subdomain if c < 16, of the own one if c < 32, else of the next one; a row may name a block more than once. Each value once; block i belongs to aggregate agg_one[i] // 2. Each value once; level-two block m belongs to aggregate agg_two[m] // 2.
All inputs are finite; a program needn't handle non-finite values.
Results may differ from the reference program's by a relative error of at most 0.0003.
Values sent between devices are 32-bit elements; how exact they have to be, the bound alone decides.
A program may use at most 128 MiB of HBM per device.

```python
from functools import partial
import jax
import jax.numpy as jnp
from jax import lax

BS = 64
NB = 16
K = 27
S2 = 3
S3 = 4
NC2 = 8
NC3 = 4
N_GRP = 64
N_DOM = 2


def draw_op_blocks(key, part):
    noise_key, center_key = jax.random.split(key)
    shape = (N_GRP, N_DOM * NB, BS, K * BS)
    spread = 1.5 * float(K * BS) ** (-0.5)
    noise = jnp.clip(jax.random.normal(noise_key, shape, jnp.float32), -5.0, 5.0) * spread
    center = jax.random.uniform(center_key, (N_GRP, N_DOM * NB, BS, 1), jnp.float32, 1.5, 3.0)
    return noise + center * jnp.eye(BS, K * BS, dtype=jnp.float32)


def draw_block_cols(key, part):
    shape = (N_GRP, N_DOM * NB, K)
    picks = jax.random.randint(key, shape, 0, 3 * NB, dtype=jnp.int32)
    rows = jnp.arange(N_DOM * NB, dtype=jnp.int32) % NB
    picks = picks.at[:, :, 0].set(NB + rows[None, :])
    picks = picks.at[:, 0, 1].set(3 * NB - 1)
    picks = picks.at[:, 1, 1].set(0)
    return picks


def restriction(key, leading, width):
    shape = leading + (BS, width)
    base = (jnp.arange(BS)[:, None] == (jnp.arange(width) % BS)[None, :]).astype(jnp.float32)
    noise = 0.01 * jnp.clip(jax.random.normal(key, shape, jnp.float32), -6.0, 6.0)
    return 0.5 * (base + noise)


def draw_restrict_one(key, part):
    return restriction(jax.random.fold_in(key, 11), (N_GRP,), N_DOM * NB * BS)


def draw_restrict_two(key, part):
    return restriction(jax.random.fold_in(key, 23), (), N_DOM * NC2 * BS)


def block_levels(stream_key, dims, cuts, low, top_value):
    loudness = 1.0
    for axis_at, parts in cuts:
        heights = jax.random.uniform(jax.random.fold_in(jax.random.fold_in(stream_key, 6), axis_at), (parts,), jnp.float32, low / len(cuts), top_value / len(cuts))
        loudness = loudness * jnp.repeat(jnp.exp(heights), dims[axis_at] // parts).reshape((-1,) + (1,) * (len(dims) - 1 - axis_at))
    return loudness


def gaussian(stream_key, dims, scale, limit, shards=(), held_as=jnp.bfloat16):
    drawn = scale * jax.random.normal(stream_key, dims, jnp.float32)
    if shards:
        drawn = drawn * block_levels(stream_key, dims, shards, -0.22, 0.18)
    return jnp.clip(drawn, -limit, limit).astype(held_as)


def setup_inputs(seed: int = 0) -> dict:
    arg_keys = jax.random.split(jax.random.key(seed), 8)
    return {
        "residual": gaussian(arg_keys[0], (N_GRP, N_DOM * NB * BS), 1.0, 6.0, ((0, 64), (1, 2)), jnp.float32),
        "op_blocks": draw_op_blocks(jax.random.fold_in(arg_keys[7], 71), 0),
        "block_cols": draw_block_cols(jax.random.fold_in(arg_keys[7], 71), 0),
        "restrict_one": draw_restrict_one(jax.random.fold_in(arg_keys[7], 71), 0),
        "restrict_two": draw_restrict_two(jax.random.fold_in(arg_keys[7], 71), 0),
        "agg_one": jax.random.permutation(arg_keys[5], NB).astype(jnp.int32),
        "agg_two": jax.random.permutation(arg_keys[6], NC2).astype(jnp.int32),
    }


HIGHEST_PREC = lax.Precision.HIGHEST
CENTER_VALUE = 2.3
HALF_WIDTH = 1.7


def chebyshev(operate, iterate, remainder, steps):
    spread_ratio = CENTER_VALUE / HALF_WIDTH
    ratio = 1.0 / spread_ratio
    direction = remainder / CENTER_VALUE
    for sweep in range(steps):
        iterate = iterate + direction
        remainder = remainder - operate(direction)
        ratio_next = 1.0 / (2.0 * spread_ratio - ratio)
        direction = (ratio_next * ratio) * direction + (2.0 * ratio_next / HALF_WIDTH) * remainder
        ratio = ratio_next
    return iterate, remainder


def coarse_rows(blocks, columns, restrict_own, restrict_wide, agg_map, fine_res):
    num_blocks = blocks.shape[0]
    block_size = blocks.shape[1]
    per_row = columns.shape[1]
    num_coarse = num_blocks // 2
    aggregate = agg_map // 2
    own_blocks = restrict_own.reshape(block_size, num_blocks, block_size).transpose(1, 0, 2)
    wide_blocks = restrict_wide.reshape(block_size, 3 * num_blocks, block_size).transpose(1, 0, 2)
    shaped = blocks.reshape(num_blocks, block_size, per_row, block_size)
    left_prod = jnp.einsum("ixy,iykz->ikxz", own_blocks, shaped, precision=HIGHEST_PREC)
    picked = jnp.take(wide_blocks, columns, axis=0)
    terms = jnp.einsum("ikxz,ikwz->ikxw", left_prod, picked, precision=HIGHEST_PREC)
    local_col = columns % num_blocks
    matches = local_col[:, :, None] == jnp.arange(num_blocks, dtype=jnp.int32)[None, None, :]
    col_aggregate = jnp.sum(jnp.where(matches, aggregate[None, None, :], 0), axis=2).astype(jnp.int32)
    target = (columns // num_blocks) * num_coarse + col_aggregate
    col_hot = (target[:, :, None] == jnp.arange(3 * num_coarse, dtype=jnp.int32)[None, None, :]).astype(jnp.float32)
    row_hot = (aggregate[None, :] == jnp.arange(num_coarse, dtype=jnp.int32)[:, None]).astype(jnp.float32)
    merged = jnp.einsum("ikc,ikxw->icxw", col_hot, terms, precision=HIGHEST_PREC)
    coarse_blk = jnp.einsum("ai,icxw->axcw", row_hot, merged, precision=HIGHEST_PREC)
    coarse_op = coarse_blk.reshape(num_coarse * block_size, 3 * num_coarse * block_size)
    local_res = jnp.einsum("ixy,iy->ix", own_blocks, fine_res.reshape(num_blocks, block_size), precision=HIGHEST_PREC)
    coarse_res = jnp.dot(row_hot, local_res, precision=HIGHEST_PREC).reshape(num_coarse * block_size)
    return coarse_op, coarse_res


def dense_restrict(restrict_blocks, agg_map):
    block_size = restrict_blocks.shape[0]
    fine_count = restrict_blocks.shape[1] // block_size
    coarse_count = fine_count // 2
    owner = (agg_map[None, :] // 2 == jnp.arange(coarse_count, dtype=jnp.int32)[:, None]).astype(jnp.float32)
    shaped = restrict_blocks.reshape(block_size, fine_count, block_size)
    spread_out = owner[:, None, :, None] * shaped[None, :, :, :]
    return spread_out.reshape(coarse_count * block_size, fine_count * block_size)


def coarse_three(coarse_op, restrict_prev, restrict_mid, restrict_next):
    size_two = coarse_op.shape[0]
    pieces = []
    for section, restrict_side in enumerate((restrict_prev, restrict_mid, restrict_next)):
        column_part = coarse_op[:, section * size_two:(section + 1) * size_two]
        inner = jnp.dot(restrict_mid, column_part, precision=HIGHEST_PREC)
        pieces.append(jnp.dot(inner, restrict_side.T, precision=HIGHEST_PREC))
    return jnp.concatenate(pieces, axis=1)


def side_concat(values, dom_axis):
    widths = [(0, 0)] * values.ndim
    widths[dom_axis] = (1, 1)
    padded = jnp.pad(values, widths)
    count = values.shape[dom_axis]
    prev_part = lax.slice_in_dim(padded, 0, count, axis=dom_axis)
    mid_part = lax.slice_in_dim(padded, 1, count + 1, axis=dom_axis)
    next_part = lax.slice_in_dim(padded, 2, count + 2, axis=dom_axis)
    return prev_part, mid_part, next_part


def apply_level(coarse_ops, vectors):
    prev_part, mid_part, next_part = side_concat(vectors, 1)
    extended = jnp.concatenate([prev_part, mid_part, next_part], axis=2)
    return jnp.einsum("pdij,pdj->pdi", coarse_ops, extended, precision=HIGHEST_PREC)


def reference(residual, op_blocks, block_cols, restrict_one, restrict_two, agg_one, agg_two):
    fine_size = NB * BS
    blocks = op_blocks.reshape(N_GRP * N_DOM, NB, BS, K * BS)
    columns = block_cols.reshape(N_GRP * N_DOM, NB, K)
    rest_one = restrict_one.reshape(N_GRP, BS, N_DOM, fine_size).transpose(0, 2, 1, 3)
    prev_part, mid_part, next_part = side_concat(rest_one, 1)
    rest_wide = jnp.concatenate([prev_part, mid_part, next_part], axis=3)
    fine_res = residual.reshape(N_GRP * N_DOM, fine_size)

    def one_device(items):
        return coarse_rows(items[0], items[1], items[2], items[3], agg_one, items[4])

    parts_op, parts_res = lax.map(one_device, (blocks, columns, rest_one.reshape(N_GRP * N_DOM, BS, fine_size), rest_wide.reshape(N_GRP * N_DOM, BS, 3 * fine_size), fine_res))
    size_two = NC2 * BS
    size_three = NC3 * BS
    pair_parts = parts_op.reshape(N_GRP // 2, 2, N_DOM, size_two, 3 * size_two)
    pair_ops = pair_parts[:, 0] + pair_parts[:, 1]
    rhs_parts = parts_res.reshape(N_GRP // 2, 2, N_DOM, size_two)
    pair_rhs = rhs_parts[:, 0] + rhs_parts[:, 1]
    level_two = partial(apply_level, pair_ops)
    smooth_two, rest_two = chebyshev(level_two, jnp.zeros_like(pair_rhs), pair_rhs, S2)
    rest_blocks = restrict_two.reshape(BS, N_DOM, size_two).transpose(1, 0, 2)
    dense = jax.vmap(dense_restrict, in_axes=(0, None))(rest_blocks, agg_two)
    dense_prev, dense_mid, dense_next = side_concat(dense, 0)
    per_dom = jax.vmap(coarse_three, in_axes=(0, 0, 0, 0))
    quad_parts = jax.vmap(per_dom, in_axes=(0, None, None, None))(pair_ops, dense_prev, dense_mid, dense_next)
    quad_parts = quad_parts.reshape(N_GRP // 4, 2, N_DOM, size_three, 3 * size_three)
    quad_ops = quad_parts[:, 0] + quad_parts[:, 1]
    quad_res = jnp.einsum("dab,pdb->pda", dense, rest_two, precision=HIGHEST_PREC)
    quad_res = quad_res.reshape(N_GRP // 4, 2, N_DOM, size_three)
    quad_rhs = quad_res[:, 0] + quad_res[:, 1]
    level_three = partial(apply_level, quad_ops)
    coarse_sol, unused = chebyshev(level_three, jnp.zeros_like(quad_rhs), quad_rhs, S3)
    lifted = jnp.einsum("dab,pda->pdb", dense, jnp.repeat(coarse_sol, 2, axis=0), precision=HIGHEST_PREC)
    start_two = smooth_two + lifted
    final_two, unused = chebyshev(level_two, start_two, pair_rhs - level_two(start_two), S2)
    spread_two = jnp.repeat(final_two, 2, axis=0).reshape(N_GRP, N_DOM, NC2, BS)
    owner = (agg_one[:, None] // 2 == jnp.arange(NC2, dtype=jnp.int32)[None, :]).astype(jnp.float32)
    picked = jnp.einsum("ia,gdax->gdix", owner, spread_two, precision=HIGHEST_PREC)
    rest_shaped = rest_one.reshape(N_GRP, N_DOM, BS, NB, BS)
    correction = jnp.einsum("gdxiy,gdix->gdiy", rest_shaped, picked, precision=HIGHEST_PREC)
    return correction.reshape(N_GRP, N_DOM * NB * BS)
```

```python
from functools import partial

import jax
import jax.numpy as jnp
from jax import lax
from jax.experimental import pallas as pl
from jax.experimental.pallas import tpu as pltpu
from jax.sharding import PartitionSpec as P

S2 = 3
S3 = 4
CENTER_VALUE = 2.3
HALF_WIDTH = 1.7
F32 = jnp.float32
BF16 = jnp.bfloat16
MESH = pl.DeviceIdType.MESH
A_CHUNKS = 4
PAIR = ((0, 1), (1, 0), (1, 1))
QUAD = PAIR + ((2, 0), (2, 1), (3, 0), (3, 1))
N_EX = 10


def pieces(value):
    hi = value.astype(BF16)
    lo = (value - hi.astype(F32)).astype(BF16)
    return hi, lo


def mm(a, b):
    return jnp.dot(a, b, preferred_element_type=F32)


def mm_nt(a, b):
    return lax.dot_general(a, b, (((1,), (1,)), ((), ())), preferred_element_type=F32)


def kernel(
    agg1_ref,
    agg2_ref,
    res_ref,
    cols_ref,
    r2_ref,
    r1_hbm,
    a_hbm,
    out_ref,
    a_buf,
    r1_buf,
    r31_buf,
    r2_blk,
    wp_ref,
    wr_ref,
    mask_ref,
    hot_ref,
    ug_ref,
    acc_ref,
    send_buf,
    recv_buf,
    a_sem,
    r1_sem,
    rx_send,
    rx_recv,
    send_sem,
    recv_sem,
):
    g = lax.axis_index("grp")
    d = lax.axis_index("dom")

    def peer(relation):
        bits, core = relation
        chip = g
        if bits & 1:
            chip = chip + 1 - 2 * (g % 2)
        if bits & 2:
            chip = chip + 2 - 4 * ((g // 2) % 2)
        return (chip, 1 - d if core else d)

    r1_copy = pltpu.make_async_copy(r1_hbm, r1_buf.at[pl.ds(d * 64, 64)], r1_sem)
    r1_copy.start()
    a_copies = []
    rows = 1024 // A_CHUNKS
    for part in range(A_CHUNKS):
        cut = pl.ds(part * rows, rows)
        a_copies.append(pltpu.make_async_copy(a_hbm.at[cut], a_buf.at[cut], a_sem.at[part]))
        a_copies[-1].start()

    barrier = pltpu.get_barrier_semaphore()
    for relation in QUAD:
        pl.semaphore_signal(barrier, inc=1, device_id=peer(relation), device_id_type=MESH)

    lane = lax.broadcasted_iota(jnp.int32, (8, 128), 1)
    row = lax.broadcasted_iota(jnp.int32, (8, 128), 0)
    left = lane < 64
    mine = (lane // 64) == d

    aggs = []
    for j in range(16):
        a = agg1_ref[j] // 2
        aggs.append(a)
    for jj in range(8):
        first, second = aggs[2 * jj], aggs[2 * jj + 1]
        m1 = jnp.where(left, first, second) == row
        m3 = jnp.where(left, agg2_ref[first] // 2, agg2_ref[second] // 2) == row
        cut = slice(jj * 128, (jj + 1) * 128)
        mask_ref[0, :, cut] = jnp.where(m1, 1.0, 0.0).astype(F32)
        mask_ref[1, :, cut] = jnp.where(m3, 1.0, 0.0).astype(F32)

    for m in range(8):
        r2_blk[m] = r2_ref[:, m * 64 : (m + 1) * 64]

    place = cols_ref[...] + 16 * (d - 1)
    valid = (place >= 0) & (place < 32)
    half = place % 2
    inner = (place // 16) * 8 + (place % 16) // 2
    even = jnp.where(valid, half * 16 + inner, -1)
    odd = jnp.where(valid, 32 + (1 - half) * 16 + inner, -1)
    spot = lax.broadcasted_iota(jnp.int32, (16, 128), 1) % 64
    for kk in range(14):
        hit = even[:, 2 * kk : 2 * kk + 1] == spot
        if 2 * kk + 1 < 27:
            hit = hit | (odd[:, 2 * kk + 1 : 2 * kk + 2] == spot)
        hot_ref[kk * 16 : (kk + 1) * 16, :] = jnp.where(hit, 1.0, 0.0).astype(BF16)

    def start_sends(ex, relations):
        copies = []
        for relation in relations:
            slot = QUAD.index(relation)
            copy = pltpu.make_async_remote_copy(
                src_ref=send_buf.at[ex],
                dst_ref=recv_buf.at[ex, slot],
                send_sem=send_sem.at[ex, slot],
                recv_sem=recv_sem.at[ex, slot],
                device_id=peer(relation),
                device_id_type=MESH,
            )
            copy.start()
            copies.append(copy)
        return copies

    started = []

    def own(value):
        return jnp.where(mine, value, 0.0)

    def send(ex, low, high, relations):
        send_buf[ex, 0:8] = own(low)
        if high is not None:
            send_buf[ex, 8:16] = own(high)
        copies = start_sends(ex, relations)
        started.extend(copies)
        return copies

    def total(ex, copies, relations, base, relations_used):
        slots = [QUAD.index(relation) for relation in relations_used]
        value = send_buf[ex, base : base + 8]
        for slot in slots:
            value = value + recv_buf[ex, slot, base : base + 8]
        return value

    def restrict(y):
        hi1, lo1 = pieces(y * mask_ref[0])
        hi3, lo3 = pieces(y * mask_ref[1])
        out = mm(jnp.concatenate([hi1, lo1, hi3, lo3], axis=0), wr_ref[...])
        s1 = out[0:8, 0:128] + out[8:16, 0:128]
        s3 = out[16:24, 128:256] + out[24:32, 128:256]
        return s1 + pltpu.roll(s1, 64, 1), s3 + pltpu.roll(s3, 64, 1)

    def prolong(v, level):
        v0 = jnp.where(left, v, 0.0)
        both = jnp.concatenate([v0, v - v0], axis=0)
        hi, lo = pieces(both)
        lhs = jnp.concatenate(
            [
                jnp.concatenate([hi, hi], axis=1),
                jnp.concatenate([lo, jnp.zeros_like(lo)], axis=1),
            ],
            axis=0,
        )
        prod = mm(lhs, wp_ref[level])
        prod = prod[0:16] + prod[16:32]
        rows_out = []
        for dd in range(2):
            for jj in range(8):
                cut = slice(jj * 128, (jj + 1) * 128)
                tile = prod[dd * 8 : dd * 8 + 8, cut] * mask_ref[level, :, cut]
                rows_out.append(jnp.sum(tile, axis=0, keepdims=True))
        return jnp.concatenate(rows_out, axis=0)

    def apply(v, level):
        u = prolong(v, level)
        turned = pltpu.roll(u, 64, 1)
        left16 = lax.broadcasted_iota(jnp.int32, (16, 128), 1) < 64
        spread = jnp.concatenate(
            [
                jnp.where(left16, u, 0.0),
                jnp.where(left16, turned, 0.0),
                jnp.where(left16, 0.0, u),
                jnp.where(left16, 0.0, turned),
            ],
            axis=0,
        )
        hi, lo = pieces(spread)
        gathered = mm(hot_ref[...], jnp.concatenate([hi, lo], axis=0))
        ug_ref[...] = gathered

        def block(i, carry):
            base = pl.multiple_of(i * 64, 64)
            acc = jnp.zeros((64, 128), F32)
            for kk in range(13):
                acc = acc + a_buf[pl.ds(base, 64), kk * 128 : (kk + 1) * 128] * ug_ref[
                    pl.ds(kk * 16 + i, 1), :
                ]
            tail = a_buf[pl.ds(base, 64), 1664:1728] * ug_ref[pl.ds(13 * 16 + i, 1), 0:64]
            acc = acc + jnp.concatenate([tail, jnp.zeros((64, 64), F32)], axis=1)
            acc_hi, acc_lo = pieces(acc)
            acc_ref[pl.ds(base, 64), 0:128] = acc_hi
            acc_ref[pl.ds(base, 64), 128:256] = acc_lo
            return carry

        lax.fori_loop(0, 16, block, 0, unroll=2)
        y = mm_nt(jnp.ones((16, 256), BF16), acc_ref[...])
        return restrict(y[0:8])

    r1_copy.wait()
    own_r1 = r1_buf[pl.ds(pl.multiple_of(d * 64, 64), 64), :]
    hi, lo = pieces(own_r1.T)
    wr_ref[:, 0:64] = hi
    wr_ref[:, 64:128] = lo
    wr_ref[:, 128:256] = jnp.zeros((1024, 128), BF16)

    pl.semaphore_wait(barrier, len(QUAD))

    def swap_copy(buf, index):
        ref = buf.at[pl.ds(d * 64, 64)]
        return pltpu.make_async_remote_copy(
            src_ref=ref,
            dst_ref=ref,
            send_sem=rx_send.at[index],
            recv_sem=rx_recv.at[index],
            device_id=(g, 1 - d),
            device_id_type=MESH,
        )

    swap1 = swap_copy(r1_buf, 0)
    swap1.start()

    y0 = jnp.broadcast_to(res_ref[...], (8, 1024))
    w, unused = restrict(y0)
    copies = send(0, w, None, PAIR)

    for jj in range(8):
        parts = []
        for half_at in range(2):
            j = 2 * jj + half_at
            parts.append(
                jnp.dot(
                    r2_blk[aggs[j]],
                    own_r1[:, j * 64 : (j + 1) * 64],
                    preferred_element_type=F32,
                    precision=lax.Precision.HIGHEST,
                )
            )
        r31_buf[pl.ds(pl.multiple_of(d * 64, 64), 64), jj * 128 : (jj + 1) * 128] = jnp.concatenate(
            parts, axis=1
        )
    own_r31 = r31_buf[pl.ds(pl.multiple_of(d * 64, 64), 64), :]
    swap3 = swap_copy(r31_buf, 1)
    swap3.start()
    hi, lo = pieces(own_r31.T)
    wr_ref[:, 128:192] = hi
    wr_ref[:, 192:256] = lo
    unused, coarse = restrict(y0)

    swap1.wait()
    hi, lo = pieces(r1_buf[...])
    wp_ref[0, 0:128] = hi
    wp_ref[0, 128:256] = lo

    for copy in a_copies:
        copy.wait()

    spread_ratio = CENTER_VALUE / HALF_WIDTH

    def wait_all(copies):
        for copy in copies:
            copy.wait_recv()

    def pair_total(ex, copies):
        wait_all(copies)
        return total(ex, copies, PAIR, 0, PAIR)

    def quad_total(ex, copies, base=0):
        wait_all(copies)
        return total(ex, copies, QUAD, base, QUAD)

    rest = pair_total(0, copies)
    start = jnp.zeros((8, 128), F32)
    direction = rest / CENTER_VALUE
    ratio = 1.0 / spread_ratio
    for sweep in range(S2):
        ex = 1 + sweep
        start = start + direction
        w, w3 = apply(direction, 0)
        coarse = coarse - w3
        if sweep == S2 - 1:
            copies = send(ex, w, coarse, QUAD)
            if True:
                swap3.wait()
                hi, lo = pieces(r31_buf[...])
                wp_ref[1, 0:128] = hi
                wp_ref[1, 128:256] = lo
            wait_all(copies)
            rest = rest - total(ex, copies, QUAD, 0, PAIR)
            rhs3 = total(ex, copies, QUAD, 8, QUAD)
        else:
            copies = send(ex, w, None, PAIR)
            rest = rest - pair_total(ex, copies)
            ratio_next = 1.0 / (2.0 * spread_ratio - ratio)
            direction = ratio_next * ratio * direction + 2.0 * ratio_next / HALF_WIDTH * rest
            ratio = ratio_next

    rest3 = rhs3
    coarse_sol = jnp.zeros((8, 128), F32)
    direction = rest3 / CENTER_VALUE
    ratio = 1.0 / spread_ratio
    for sweep in range(S3):
        coarse_sol = coarse_sol + direction
        if sweep < S3 - 1:
            ex = 1 + S2 + sweep
            unused, w3 = apply(direction, 1)
            copies = send(ex, w3, None, QUAD)
            rest3 = rest3 - quad_total(ex, copies)
            ratio_next = 1.0 / (2.0 * spread_ratio - ratio)
            direction = ratio_next * ratio * direction + 2.0 * ratio_next / HALF_WIDTH * rest3
            ratio = ratio_next

    ex = S2 + S3
    w, unused = apply(coarse_sol, 1)
    copies = send(ex, w, None, PAIR)
    rest = rest - pair_total(ex, copies)
    direction = rest / CENTER_VALUE
    ratio = 1.0 / spread_ratio
    for sweep in range(S2):
        start = start + direction
        if sweep < S2 - 1:
            ex = S2 + S3 + 1 + sweep
            w, unused = apply(direction, 0)
            copies = send(ex, w, None, PAIR)
            rest = rest - pair_total(ex, copies)
            ratio_next = 1.0 / (2.0 * spread_ratio - ratio)
            direction = ratio_next * ratio * direction + 2.0 * ratio_next / HALF_WIDTH * rest
            ratio = ratio_next

    fine = prolong(start, 0) + prolong(coarse_sol, 1)
    out_ref[...] = jnp.where(d == 0, fine[0:8], fine[8:16])

    swap_done = [copy.wait_send() for copy in started]


def body(residual, op_blocks, block_cols, restrict_one, restrict_two, agg_one, agg_two):
    vmem = pl.BlockSpec(memory_space=pltpu.VMEM)
    smem = pl.BlockSpec(memory_space=pltpu.SMEM)
    anywhere = pl.BlockSpec(memory_space=pl.ANY)
    out = pl.pallas_call(
        kernel,
        out_shape=jax.ShapeDtypeStruct((8, 128), F32),
        in_specs=[smem, smem, vmem, vmem, vmem, anywhere, anywhere],
        out_specs=vmem,
        scratch_shapes=[
            pltpu.VMEM((1024, 1728), F32),
            pltpu.VMEM((128, 1024), F32),
            pltpu.VMEM((128, 1024), F32),
            pltpu.VMEM((8, 64, 64), F32),
            pltpu.VMEM((2, 256, 1024), BF16),
            pltpu.VMEM((1024, 256), BF16),
            pltpu.VMEM((2, 8, 1024), F32),
            pltpu.VMEM((224, 128), BF16),
            pltpu.VMEM((224, 128), F32),
            pltpu.VMEM((1024, 256), BF16),
            pltpu.VMEM((N_EX, 16, 128), F32),
            pltpu.VMEM((N_EX, len(QUAD), 16, 128), F32),
            pltpu.SemaphoreType.DMA((A_CHUNKS,)),
            pltpu.SemaphoreType.DMA,
            pltpu.SemaphoreType.DMA((2,)),
            pltpu.SemaphoreType.DMA((2,)),
            pltpu.SemaphoreType.DMA((N_EX, len(QUAD))),
            pltpu.SemaphoreType.DMA((N_EX, len(QUAD))),
        ],
        compiler_params=pltpu.CompilerParams(
            collective_id=0, has_side_effects=True, vmem_limit_bytes=48 * 1024 * 1024
        ),
        cost_estimate=pl.CostEstimate(
            flops=40_000_000, bytes_accessed=7_500_000, transcendentals=0
        ),
    )(
        agg_one,
        agg_two,
        residual,
        block_cols[0],
        restrict_two,
        restrict_one[0],
        op_blocks.reshape(1024, 1728),
    )
    return out.reshape(1, 1024)


def solution(mesh):
    placed = (
        P("grp", "dom"),
        P("grp", "dom", None, None),
        P("grp", "dom", None),
        P("grp", None, "dom"),
        P(None, "dom"),
        P(),
        P(),
    )
    return jax.shard_map(
        body, mesh=mesh, in_specs=placed, out_specs=P("grp", "dom"), check_vma=False
    )
```

```python
from functools import partial

import jax
import jax.numpy as jnp
from jax import lax
from jax.experimental import pallas as pl
from jax.experimental.pallas import tpu as pltpu
from jax.sharding import PartitionSpec as P

S2 = 3
S3 = 4
CENTER_VALUE = 2.3
HALF_WIDTH = 1.7
F32 = jnp.float32
BF16 = jnp.bfloat16
MESH = pl.DeviceIdType.MESH
A_CHUNKS = 4
PAIR = ((1, 0), (1, 1), (0, 1))
QUAD = ((2, 0), (3, 0), (2, 1), (3, 1)) + PAIR
N_EX = 10


def pieces(value):
    hi = value.astype(BF16)
    lo = (value - hi.astype(F32)).astype(BF16)
    return hi, lo


def mm(a, b):
    return jnp.dot(a, b, preferred_element_type=F32)


def mm_nt(a, b):
    return lax.dot_general(a, b, (((1,), (1,)), ((), ())), preferred_element_type=F32)


def kernel(
    agg1_hbm,
    agg2_hbm,
    res_hbm,
    cols_hbm,
    r2_hbm,
    r1_hbm,
    a_hbm,
    out_ref,
    agg1_ref,
    agg2_ref,
    res_ref,
    cols_ref,
    r2_ref,
    a_buf,
    r1_buf,
    r31_buf,
    r2_blk,
    wp_ref,
    wr_ref,
    mask_ref,
    table_ref,
    send_buf,
    recv_buf,
    a_sem,
    r1_sem,
    in_sem,
    rx_send,
    rx_recv,
    send_sem,
    recv_sem,
):
    g = lax.axis_index("grp")
    d = lax.axis_index("dom")

    def peer(relation):
        bits, core = relation
        chip = g
        if bits & 1:
            chip = chip + 1 - 2 * (g % 2)
        if bits & 2:
            chip = chip + 2 - 4 * ((g // 2) % 2)
        return (chip, 1 - d if core else d)

    r1_copy = pltpu.make_async_copy(r1_hbm, r1_buf.at[pl.ds(d * 64, 64)], r1_sem)
    r1_copy.start()
    inputs = []
    for index, (source, target) in enumerate(
        (
            (agg1_hbm, agg1_ref),
            (agg2_hbm, agg2_ref),
            (cols_hbm, cols_ref),
            (res_hbm, res_ref),
            (r2_hbm, r2_ref),
        )
    ):
        inputs.append(pltpu.make_async_copy(source, target, in_sem.at[index]))
        inputs[-1].start()
    a_copies = []
    rows = 1024 // A_CHUNKS
    for part in range(A_CHUNKS):
        cut = pl.ds(part * rows, rows)
        a_copies.append(pltpu.make_async_copy(a_hbm.at[cut], a_buf.at[cut], a_sem.at[part]))
        a_copies[-1].start()

    barrier = pltpu.get_barrier_semaphore()
    for relation in QUAD:
        pl.semaphore_signal(barrier, inc=1, device_id=peer(relation), device_id_type=MESH)

    lane = lax.broadcasted_iota(jnp.int32, (8, 128), 1)
    row = lax.broadcasted_iota(jnp.int32, (8, 128), 0)
    left = lane < 64
    mine = (lane // 64) == d

    for copy in inputs:
        copy.wait()

    aggs = []
    for j in range(16):
        a = agg1_ref[j] // 2
        aggs.append(a)
    for jj in range(8):
        first, second = aggs[2 * jj], aggs[2 * jj + 1]
        m1 = jnp.where(left, first, second) == row
        m3 = jnp.where(left, agg2_ref[first] // 2, agg2_ref[second] // 2) == row
        cut = slice(jj * 128, (jj + 1) * 128)
        mask_ref[0, :, cut] = jnp.where(m1, 1.0, 0.0).astype(F32)
        mask_ref[1, :, cut] = jnp.where(m3, 1.0, 0.0).astype(F32)

    for m in range(8):
        r2_blk[m] = r2_ref[:, m * 64 : (m + 1) * 64]

    for entry in range(16):
        table_ref[0, 32 * d + entry] = jnp.zeros((8, 128), F32)
        table_ref[1, 32 * d + entry] = jnp.zeros((8, 128), F32)

    def start_sends(ex, relations):
        copies = []
        for relation in relations:
            slot = QUAD.index(relation)
            copy = pltpu.make_async_remote_copy(
                src_ref=send_buf.at[ex],
                dst_ref=recv_buf.at[ex, slot],
                send_sem=send_sem.at[ex, slot],
                recv_sem=recv_sem.at[ex, slot],
                device_id=peer(relation),
                device_id_type=MESH,
            )
            copy.start()
            copies.append(copy)
        return copies

    started = []

    def own(value):
        return jnp.where(mine, value, 0.0)

    def send(ex, low, high, relations):
        send_buf[ex, 0:8] = own(low)
        if high is not None:
            send_buf[ex, 8:16] = own(high)
        copies = start_sends(ex, relations)
        started.extend(copies)
        return copies

    def total(ex, copies, relations, base, relations_used):
        slots = [QUAD.index(relation) for relation in relations_used]
        value = send_buf[ex, base : base + 8]
        for slot in slots:
            value = value + recv_buf[ex, slot, base : base + 8]
        return value

    def restrict_part(y, group, rows):
        cut = slice(group * rows, (group + 1) * rows)
        hi1, lo1 = pieces(y * mask_ref[0, :, cut])
        hi3, lo3 = pieces(y * mask_ref[1, :, cut])
        return mm(jnp.concatenate([hi1, lo1, hi3, lo3], axis=0), wr_ref[cut])

    def restrict_end(out):
        s1 = out[0:8, 0:128] + out[8:16, 0:128]
        s3 = out[16:24, 128:256] + out[24:32, 128:256]
        return s1 + pltpu.roll(s1, 64, 1), s3 + pltpu.roll(s3, 64, 1)

    def restrict(y):
        return restrict_end(restrict_part(y, 0, 1024))

    def prolong(v, level):
        v0 = jnp.where(left, v, 0.0)
        both = jnp.concatenate([v0, v - v0], axis=0)
        hi, lo = pieces(both)
        lhs = jnp.concatenate(
            [
                jnp.concatenate([hi, hi], axis=1),
                jnp.concatenate([lo, jnp.zeros_like(lo)], axis=1),
            ],
            axis=0,
        )
        tiles = [[], []]
        for quarter in range(4):
            prod = mm(lhs, wp_ref[level, :, quarter * 256 : (quarter + 1) * 256])
            prod = prod[0:16] + prod[16:32]
            for dd in range(2):
                for part in range(2):
                    jj = 2 * quarter + part
                    tile = prod[dd * 8 : dd * 8 + 8, part * 128 : (part + 1) * 128]
                    tile = tile * mask_ref[level, :, jj * 128 : (jj + 1) * 128]
                    tile = tile + pltpu.roll(tile, 4, 0)
                    tile = tile + pltpu.roll(tile, 2, 0)
                    tile = tile + pltpu.roll(tile, 1, 0)
                    tiles[dd].append(tile)
        return tiles

    def own_rows(tiles):
        value = jnp.zeros((8, 128), F32)
        for jj in range(8):
            value = jnp.where(row == jj, jnp.where(d == 0, tiles[0][jj], tiles[1][jj]), value)
        return value

    def apply(v, level):
        tiles = prolong(v, level)
        for dd in range(2):
            base = (dd - d + 1) * 16
            for jj in range(8):
                tile = tiles[dd][jj]
                turned = pltpu.roll(tile, 64, 1)
                table_ref[0, base + 2 * jj] = tile
                table_ref[1, base + 2 * jj + 1] = tile
                table_ref[0, base + 2 * jj + 1] = turned
                table_ref[1, base + 2 * jj] = turned
        out = None
        for group in range(4):
            sums = []
            for i in range(group * 4, group * 4 + 4):
                base = i * 64
                acc = jnp.zeros((8, 8, 128), F32)
                for kk in range(13):
                    u = jnp.where(
                        left, table_ref[0, cols_ref[i, 2 * kk]], table_ref[1, cols_ref[i, 2 * kk + 1]]
                    )
                    block = a_buf[base : base + 64, kk * 128 : (kk + 1) * 128]
                    acc = acc + block.reshape(8, 8, 128) * u[None]
                u = table_ref[0, cols_ref[i, 26]]
                tail = a_buf[base : base + 64, 1664:1728].reshape(8, 8, 64) * u[None, :, 0:64]
                acc = acc + jnp.concatenate([tail, jnp.zeros((8, 8, 64), F32)], axis=2)
                acc_hi, acc_lo = pieces(acc.reshape(64, 128))
                sums.append(jnp.concatenate([acc_hi, acc_lo], axis=1))
            y = mm_nt(jnp.ones((16, 256), BF16), jnp.concatenate(sums, axis=0))
            part = restrict_part(y[0:8], group, 256)
            out = part if out is None else out + part
        return restrict_end(out)

    r1_copy.wait()
    own_r1 = r1_buf[pl.ds(pl.multiple_of(d * 64, 64), 64), :]
    hi, lo = pieces(own_r1.T)
    wr_ref[:, 0:64] = hi
    wr_ref[:, 64:128] = lo
    wr_ref[:, 128:256] = jnp.zeros((1024, 128), BF16)

    pl.semaphore_wait(barrier, len(QUAD))

    def swap_copy(buf, index):
        ref = buf.at[pl.ds(d * 64, 64)]
        return pltpu.make_async_remote_copy(
            src_ref=ref,
            dst_ref=ref,
            send_sem=rx_send.at[index],
            recv_sem=rx_recv.at[index],
            device_id=(g, 1 - d),
            device_id_type=MESH,
        )

    swap1 = swap_copy(r1_buf, 0)
    swap1.start()

    y0 = jnp.broadcast_to(res_ref[...], (8, 1024))
    w, unused = restrict(y0)
    copies = send(0, w, None, PAIR)

    for jj in range(8):
        parts = []
        for half_at in range(2):
            j = 2 * jj + half_at
            parts.append(
                jnp.dot(
                    r2_blk[aggs[j]],
                    own_r1[:, j * 64 : (j + 1) * 64],
                    preferred_element_type=F32,
                    precision=lax.Precision.HIGHEST,
                )
            )
        r31_buf[pl.ds(pl.multiple_of(d * 64, 64), 64), jj * 128 : (jj + 1) * 128] = jnp.concatenate(
            parts, axis=1
        )
    own_r31 = r31_buf[pl.ds(pl.multiple_of(d * 64, 64), 64), :]
    swap3 = swap_copy(r31_buf, 1)
    swap3.start()
    hi, lo = pieces(own_r31.T)
    wr_ref[:, 128:192] = hi
    wr_ref[:, 192:256] = lo
    unused, coarse = restrict(y0)

    swap1.wait()
    hi, lo = pieces(r1_buf[...])
    wp_ref[0, 0:128] = hi
    wp_ref[0, 128:256] = lo

    for copy in a_copies:
        copy.wait()

    spread_ratio = CENTER_VALUE / HALF_WIDTH

    def wait_all(copies):
        for copy in copies:
            copy.wait_recv()

    def pair_total(ex, copies):
        wait_all(copies)
        return total(ex, copies, PAIR, 0, PAIR)

    def quad_total(ex, copies, base=0):
        wait_all(copies)
        return total(ex, copies, QUAD, base, QUAD)

    rest = pair_total(0, copies)
    start = jnp.zeros((8, 128), F32)
    direction = rest / CENTER_VALUE
    ratio = 1.0 / spread_ratio
    for sweep in range(S2):
        ex = 1 + sweep
        start = start + direction
        w, w3 = apply(direction, 0)
        coarse = coarse - w3
        if sweep == S2 - 1:
            copies = send(ex, w, coarse, QUAD)
            swap3.wait()
            hi, lo = pieces(r31_buf[...])
            wp_ref[1, 0:128] = hi
            wp_ref[1, 128:256] = lo
            wait_all(copies)
            rest = rest - total(ex, copies, QUAD, 0, PAIR)
            rhs3 = total(ex, copies, QUAD, 8, QUAD)
        else:
            copies = send(ex, w, None, PAIR)
            rest = rest - pair_total(ex, copies)
            ratio_next = 1.0 / (2.0 * spread_ratio - ratio)
            direction = ratio_next * ratio * direction + 2.0 * ratio_next / HALF_WIDTH * rest
            ratio = ratio_next

    rest3 = rhs3
    coarse_sol = jnp.zeros((8, 128), F32)
    direction = rest3 / CENTER_VALUE
    ratio = 1.0 / spread_ratio
    for sweep in range(S3):
        coarse_sol = coarse_sol + direction
        if sweep < S3 - 1:
            ex = 1 + S2 + sweep
            unused, w3 = apply(direction, 1)
            copies = send(ex, w3, None, QUAD)
            rest3 = rest3 - quad_total(ex, copies)
            ratio_next = 1.0 / (2.0 * spread_ratio - ratio)
            direction = ratio_next * ratio * direction + 2.0 * ratio_next / HALF_WIDTH * rest3
            ratio = ratio_next

    ex = S2 + S3
    w, unused = apply(coarse_sol, 1)
    copies = send(ex, w, None, PAIR)
    fine_coarse = own_rows(prolong(coarse_sol, 1))
    rest = rest - pair_total(ex, copies)
    direction = rest / CENTER_VALUE
    ratio = 1.0 / spread_ratio
    for sweep in range(S2):
        start = start + direction
        if sweep < S2 - 1:
            ex = S2 + S3 + 1 + sweep
            w, unused = apply(direction, 0)
            copies = send(ex, w, None, PAIR)
            rest = rest - pair_total(ex, copies)
            ratio_next = 1.0 / (2.0 * spread_ratio - ratio)
            direction = ratio_next * ratio * direction + 2.0 * ratio_next / HALF_WIDTH * rest
            ratio = ratio_next

    out_ref[...] = own_rows(prolong(start, 0)) + fine_coarse

    for copy in started:
        copy.wait_send()


def body(residual, op_blocks, block_cols, restrict_one, restrict_two, agg_one, agg_two):
    vmem = pl.BlockSpec(memory_space=pltpu.VMEM)
    hbm = pl.BlockSpec(memory_space=pltpu.HBM)
    out = pl.pallas_call(
        kernel,
        out_shape=jax.ShapeDtypeStruct((8, 128), F32),
        in_specs=[hbm] * 7,
        out_specs=vmem,
        scratch_shapes=[
            pltpu.SMEM((16,), jnp.int32),
            pltpu.SMEM((8,), jnp.int32),
            pltpu.VMEM((1, 1024), F32),
            pltpu.SMEM((16, 27), jnp.int32),
            pltpu.VMEM((64, 512), F32),
            pltpu.VMEM((1024, 1728), F32),
            pltpu.VMEM((128, 1024), F32),
            pltpu.VMEM((128, 1024), F32),
            pltpu.VMEM((8, 64, 64), F32),
            pltpu.VMEM((2, 256, 1024), BF16),
            pltpu.VMEM((1024, 256), BF16),
            pltpu.VMEM((2, 8, 1024), F32),
            pltpu.VMEM((2, 48, 8, 128), F32),
            pltpu.VMEM((N_EX, 16, 128), F32),
            pltpu.VMEM((N_EX, len(QUAD), 16, 128), F32),
            pltpu.SemaphoreType.DMA((A_CHUNKS,)),
            pltpu.SemaphoreType.DMA,
            pltpu.SemaphoreType.DMA((5,)),
            pltpu.SemaphoreType.DMA((2,)),
            pltpu.SemaphoreType.DMA((2,)),
            pltpu.SemaphoreType.DMA((N_EX, len(QUAD))),
            pltpu.SemaphoreType.DMA((N_EX, len(QUAD))),
        ],
        compiler_params=pltpu.CompilerParams(
            collective_id=0, has_side_effects=True, vmem_limit_bytes=48 * 1024 * 1024
        ),
        cost_estimate=pl.CostEstimate(
            flops=40_000_000, bytes_accessed=7_500_000, transcendentals=0
        ),
    )(
        *(
            pltpu.with_memory_space_constraint(value, pltpu.HBM)
            for value in (
                agg_one,
                agg_two,
                residual,
                block_cols[0],
                restrict_two,
                restrict_one[0],
                op_blocks.reshape(1024, 1728),
            )
        )
    )
    return out.reshape(1, 1024)


def solution(mesh):
    placed = (
        P("grp", "dom"),
        P("grp", "dom", None, None),
        P("grp", "dom", None),
        P("grp", None, "dom"),
        P(None, "dom"),
        P(),
        P(),
    )
    return jax.shard_map(
        body, mesh=mesh, in_specs=placed, out_specs=P("grp", "dom"), check_vma=False
    )
```

```python
from functools import partial

import jax
import jax.numpy as jnp
from jax import lax
from jax.experimental import pallas as pl
from jax.experimental.pallas import tpu as pltpu
from jax.sharding import PartitionSpec as P

S2 = 3
S3 = 4
CENTER_VALUE = 2.3
HALF_WIDTH = 1.7
F32 = jnp.float32
BF16 = jnp.bfloat16
MESH = pl.DeviceIdType.MESH
A_CHUNKS = 4
PAIR = ((1, 0), (1, 1), (0, 1))
QUAD = ((2, 0), (3, 0), (2, 1), (3, 1)) + PAIR
N_EX = 10


def pieces(value):
    hi = value.astype(BF16)
    lo = (value - hi.astype(F32)).astype(BF16)
    return hi, lo


def mm(a, b):
    return jnp.dot(a, b, preferred_element_type=F32)


def kernel(
    agg1_hbm,
    agg2_hbm,
    res_hbm,
    cols_hbm,
    r2_hbm,
    r1_hbm,
    a_hbm,
    out_ref,
    agg1_ref,
    agg2_ref,
    res_ref,
    cols_ref,
    r2_ref,
    a_buf,
    r1_buf,
    r31_buf,
    r2_blk,
    wp_ref,
    wr_ref,
    mask_ref,
    hot_ref,
    ug_ref,
    rt_ref,
    pick_ref,
    send_buf,
    recv_buf,
    a_sem,
    r1_sem,
    in_sem,
    rx_send,
    rx_recv,
    send_sem,
    recv_sem,
):
    g = lax.axis_index("grp")
    d = lax.axis_index("dom")

    def peer(relation):
        bits, core = relation
        chip = g
        if bits & 1:
            chip = chip + 1 - 2 * (g % 2)
        if bits & 2:
            chip = chip + 2 - 4 * ((g // 2) % 2)
        return (chip, 1 - d if core else d)

    r1_copy = pltpu.make_async_copy(r1_hbm, r1_buf.at[pl.ds(d * 64, 64)], r1_sem)
    r1_copy.start()
    inputs = []
    for index, (source, target) in enumerate(
        (
            (agg1_hbm, agg1_ref),
            (agg2_hbm, agg2_ref),
            (cols_hbm, cols_ref),
            (res_hbm, res_ref),
            (r2_hbm, r2_ref),
        )
    ):
        inputs.append(pltpu.make_async_copy(source, target, in_sem.at[index]))
        inputs[-1].start()
    a_copies = []
    rows = 1024 // A_CHUNKS
    for part in range(A_CHUNKS):
        cut = pl.ds(part * rows, rows)
        a_copies.append(pltpu.make_async_copy(a_hbm.at[cut], a_buf.at[cut], a_sem.at[part]))
        a_copies[-1].start()

    barrier = pltpu.get_barrier_semaphore()
    for relation in QUAD:
        pl.semaphore_signal(barrier, inc=1, device_id=peer(relation), device_id_type=MESH)

    lane = lax.broadcasted_iota(jnp.int32, (8, 128), 1)
    row = lax.broadcasted_iota(jnp.int32, (8, 128), 0)
    left = lane < 64
    mine = (lane // 64) == d

    for copy in inputs:
        copy.wait()

    aggs = []
    for j in range(16):
        a = agg1_ref[j] // 2
        aggs.append(a)
    for jj in range(8):
        first, second = aggs[2 * jj], aggs[2 * jj + 1]
        m1 = jnp.where(left, first, second) == row
        m3 = jnp.where(left, agg2_ref[first] // 2, agg2_ref[second] // 2) == row
        cut = slice(jj * 128, (jj + 1) * 128)
        mask_ref[0, :, cut] = jnp.where(m1, 1.0, 0.0).astype(F32)
        mask_ref[1, :, cut] = jnp.where(m3, 1.0, 0.0).astype(F32)

    for j in range(16):
        pick_ref[j] = jnp.where(jnp.where(left, aggs[j], agg2_ref[aggs[j]] // 2) == row, 1.0, 0.0)

    for m in range(8):
        r2_blk[m] = r2_ref[:, m * 64 : (m + 1) * 64]

    place = cols_ref[...] + 16 * (d - 1)
    valid = (place >= 0) & (place < 32)
    half = place % 2
    inner = (place // 16) * 8 + (place % 16) // 2
    even = jnp.where(valid, half * 16 + inner, -1)
    odd = jnp.where(valid, 32 + (1 - half) * 16 + inner, -1)
    spot = lax.broadcasted_iota(jnp.int32, (16, 128), 1) % 64
    for kk in range(14):
        hit = even[:, 2 * kk : 2 * kk + 1] == spot
        if 2 * kk + 1 < 27:
            hit = hit | (odd[:, 2 * kk + 1 : 2 * kk + 2] == spot)
        hot_ref[kk * 16 : (kk + 1) * 16, :] = jnp.where(hit, 1.0, 0.0).astype(BF16)

    def start_sends(ex, relations, rows):
        copies = []
        for relation in relations:
            slot = QUAD.index(relation)
            copy = pltpu.make_async_remote_copy(
                src_ref=send_buf.at[ex, 0:rows],
                dst_ref=recv_buf.at[ex, slot, 0:rows],
                send_sem=send_sem.at[ex, slot],
                recv_sem=recv_sem.at[ex, slot],
                device_id=peer(relation),
                device_id_type=MESH,
            )
            copy.start()
            copies.append(copy)
        return copies

    started = []

    def own(value):
        return jnp.where(mine, value, 0.0)

    def send(ex, low, high, relations):
        send_buf[ex, 0:8] = own(low)
        if high is not None:
            send_buf[ex, 8:16] = own(high)
        copies = start_sends(ex, relations, 8 if high is None else 16)
        started.extend(copies)
        return copies

    def total(ex, copies, relations, base, relations_used):
        slots = [QUAD.index(relation) for relation in relations_used]
        value = send_buf[ex, base : base + 8]
        for slot in slots:
            value = value + recv_buf[ex, slot, base : base + 8]
        return value

    def restrict_part(y, group, rows):
        cut = slice(group * rows, (group + 1) * rows)
        hi1, lo1 = pieces(y * mask_ref[0, :, cut])
        hi3, lo3 = pieces(y * mask_ref[1, :, cut])
        return mm(jnp.concatenate([hi1, lo1, hi3, lo3], axis=0), wr_ref[cut])

    def restrict_end(out):
        s1 = out[0:8, 0:128] + out[8:16, 0:128]
        s3 = out[16:24, 128:256] + out[24:32, 128:256]
        return s1 + pltpu.roll(s1, 64, 1), s3 + pltpu.roll(s3, 64, 1)

    def restrict(y):
        return restrict_end(restrict_part(y, 0, 1024))

    def prolong(v, level):
        v0 = jnp.where(left, v, 0.0)
        both = jnp.concatenate([v0, v - v0], axis=0)
        hi, lo = pieces(both)
        lhs = jnp.concatenate(
            [
                jnp.concatenate([hi, hi], axis=1),
                jnp.concatenate([lo, jnp.zeros_like(lo)], axis=1),
            ],
            axis=0,
        )
        tiles = [[], []]
        for quarter in range(4):
            prod = mm(lhs, wp_ref[level, :, quarter * 256 : (quarter + 1) * 256])
            prod = prod[0:16] + prod[16:32]
            for dd in range(2):
                for part in range(2):
                    jj = 2 * quarter + part
                    tile = prod[dd * 8 : dd * 8 + 8, part * 128 : (part + 1) * 128]
                    tile = tile * mask_ref[level, :, jj * 128 : (jj + 1) * 128]
                    tile = tile + pltpu.roll(tile, 4, 0)
                    tile = tile + pltpu.roll(tile, 2, 0)
                    tile = tile + pltpu.roll(tile, 1, 0)
                    tiles[dd].append(tile)
        return tiles

    def rows_of(tiles):
        value = tiles[0]
        for jj in range(1, 8):
            value = jnp.where(row == jj, tiles[jj], value)
        return value

    def own_rows(tiles):
        return jnp.where(d == 0, rows_of(tiles[0]), rows_of(tiles[1]))

    def apply(v, level):
        tiles = prolong(v, level)
        u = jnp.concatenate([rows_of(tiles[0]), rows_of(tiles[1])], axis=0)
        turned = pltpu.roll(u, 64, 1)
        left16 = jnp.concatenate([left, left], axis=0)
        spread = jnp.concatenate(
            [
                jnp.where(left16, u, 0.0),
                jnp.where(left16, turned, 0.0),
                jnp.where(left16, 0.0, u),
                jnp.where(left16, 0.0, turned),
            ],
            axis=0,
        )
        hi, lo = pieces(spread)
        ug_ref[...] = mm(hot_ref[...], jnp.concatenate([hi, lo], axis=0))
        out = None
        for i in range(16):
            base = i * 64
            acc = jnp.zeros((8, 8, 128), F32)
            for kk in range(13):
                u = jnp.broadcast_to(ug_ref[kk * 16 + i : kk * 16 + i + 1, :], (8, 128))
                block = a_buf[base : base + 64, kk * 128 : (kk + 1) * 128]
                acc = acc + block.reshape(8, 8, 128) * u[None]
            u = jnp.broadcast_to(ug_ref[13 * 16 + i : 13 * 16 + i + 1, :], (8, 128))
            tail = a_buf[base : base + 64, 1664:1728].reshape(8, 8, 64) * u[None, :, 0:64]
            acc = acc + jnp.concatenate([tail, jnp.zeros((8, 8, 64), F32)], axis=2)
            y = jnp.sum(acc.reshape(64, 128), axis=1, keepdims=True)
            part = jnp.sum((rt_ref[base : base + 64, :] * y).reshape(8, 8, 128), axis=0)
            part = part + pltpu.roll(part, 4, 0)
            part = part + pltpu.roll(part, 2, 0)
            part = (part + pltpu.roll(part, 1, 0)) * pick_ref[i]
            out = part if out is None else out + part
        turned = pltpu.roll(out, 64, 1)
        return jnp.where(left, out, turned), jnp.where(left, turned, out)

    r1_copy.wait()
    own_r1 = r1_buf[pl.ds(pl.multiple_of(d * 64, 64), 64), :]
    hi, lo = pieces(own_r1.T)
    rt_ref[:, 0:64] = own_r1.T
    wr_ref[:, 0:64] = hi
    wr_ref[:, 64:128] = lo
    wr_ref[:, 128:256] = jnp.zeros((1024, 128), BF16)

    pl.semaphore_wait(barrier, len(QUAD))

    def swap_copy(buf, index):
        ref = buf.at[pl.ds(d * 64, 64)]
        return pltpu.make_async_remote_copy(
            src_ref=ref,
            dst_ref=ref,
            send_sem=rx_send.at[index],
            recv_sem=rx_recv.at[index],
            device_id=(g, 1 - d),
            device_id_type=MESH,
        )

    swap1 = swap_copy(r1_buf, 0)
    swap1.start()

    y0 = jnp.broadcast_to(res_ref[...], (8, 1024))
    w, unused = restrict(y0)
    copies = send(0, w, None, PAIR)

    for jj in range(8):
        parts = []
        for half_at in range(2):
            j = 2 * jj + half_at
            parts.append(
                jnp.dot(
                    r2_blk[aggs[j]],
                    own_r1[:, j * 64 : (j + 1) * 64],
                    preferred_element_type=F32,
                    precision=lax.Precision.HIGHEST,
                )
            )
        r31_buf[pl.ds(pl.multiple_of(d * 64, 64), 64), jj * 128 : (jj + 1) * 128] = jnp.concatenate(
            parts, axis=1
        )
    own_r31 = r31_buf[pl.ds(pl.multiple_of(d * 64, 64), 64), :]
    swap3 = swap_copy(r31_buf, 1)
    swap3.start()
    hi, lo = pieces(own_r31.T)
    rt_ref[:, 64:128] = own_r31.T
    wr_ref[:, 128:192] = hi
    wr_ref[:, 192:256] = lo
    unused, coarse = restrict(y0)

    swap1.wait()
    hi, lo = pieces(r1_buf[...])
    wp_ref[0, 0:128] = hi
    wp_ref[0, 128:256] = lo

    for copy in a_copies:
        copy.wait()

    spread_ratio = CENTER_VALUE / HALF_WIDTH

    def wait_all(copies):
        for copy in copies:
            copy.wait_recv()

    def pair_total(ex, copies):
        wait_all(copies)
        return total(ex, copies, PAIR, 0, PAIR)

    def quad_total(ex, copies, base=0):
        wait_all(copies)
        return total(ex, copies, QUAD, base, QUAD)

    rest = pair_total(0, copies)
    start = jnp.zeros((8, 128), F32)
    direction = rest / CENTER_VALUE
    ratio = 1.0 / spread_ratio
    for sweep in range(S2):
        ex = 1 + sweep
        start = start + direction
        w, w3 = apply(direction, 0)
        coarse = coarse - w3
        if sweep == S2 - 1:
            copies = send(ex, w, coarse, QUAD)
            swap3.wait()
            hi, lo = pieces(r31_buf[...])
            wp_ref[1, 0:128] = hi
            wp_ref[1, 128:256] = lo
            wait_all(copies)
            rest = rest - total(ex, copies, QUAD, 0, PAIR)
            rhs3 = total(ex, copies, QUAD, 8, QUAD)
        else:
            copies = send(ex, w, None, PAIR)
            rest = rest - pair_total(ex, copies)
            ratio_next = 1.0 / (2.0 * spread_ratio - ratio)
            direction = ratio_next * ratio * direction + 2.0 * ratio_next / HALF_WIDTH * rest
            ratio = ratio_next

    rest3 = rhs3
    coarse_sol = jnp.zeros((8, 128), F32)
    direction = rest3 / CENTER_VALUE
    ratio = 1.0 / spread_ratio
    for sweep in range(S3):
        coarse_sol = coarse_sol + direction
        if sweep < S3 - 1:
            ex = 1 + S2 + sweep
            unused, w3 = apply(direction, 1)
            copies = send(ex, w3, None, QUAD)
            rest3 = rest3 - quad_total(ex, copies)
            ratio_next = 1.0 / (2.0 * spread_ratio - ratio)
            direction = ratio_next * ratio * direction + 2.0 * ratio_next / HALF_WIDTH * rest3
            ratio = ratio_next

    ex = S2 + S3
    w, unused = apply(coarse_sol, 1)
    copies = send(ex, w, None, PAIR)
    fine_coarse = own_rows(prolong(coarse_sol, 1))
    rest = rest - pair_total(ex, copies)
    direction = rest / CENTER_VALUE
    ratio = 1.0 / spread_ratio
    for sweep in range(S2):
        start = start + direction
        if sweep < S2 - 1:
            ex = S2 + S3 + 1 + sweep
            w, unused = apply(direction, 0)
            copies = send(ex, w, None, PAIR)
            rest = rest - pair_total(ex, copies)
            ratio_next = 1.0 / (2.0 * spread_ratio - ratio)
            direction = ratio_next * ratio * direction + 2.0 * ratio_next / HALF_WIDTH * rest
            ratio = ratio_next

    out_ref[...] = own_rows(prolong(start, 0)) + fine_coarse

    for copy in started:
        copy.wait_send()


def body(residual, op_blocks, block_cols, restrict_one, restrict_two, agg_one, agg_two):
    vmem = pl.BlockSpec(memory_space=pltpu.VMEM)
    hbm = pl.BlockSpec(memory_space=pltpu.HBM)
    out = pl.pallas_call(
        kernel,
        out_shape=jax.ShapeDtypeStruct((8, 128), F32),
        in_specs=[hbm] * 7,
        out_specs=vmem,
        scratch_shapes=[
            pltpu.SMEM((16,), jnp.int32),
            pltpu.SMEM((8,), jnp.int32),
            pltpu.VMEM((1, 1024), F32),
            pltpu.VMEM((16, 27), jnp.int32),
            pltpu.VMEM((64, 512), F32),
            pltpu.VMEM((1024, 1728), F32),
            pltpu.VMEM((128, 1024), F32),
            pltpu.VMEM((128, 1024), F32),
            pltpu.VMEM((8, 64, 64), F32),
            pltpu.VMEM((2, 256, 1024), BF16),
            pltpu.VMEM((1024, 256), BF16),
            pltpu.VMEM((2, 8, 1024), F32),
            pltpu.VMEM((224, 128), BF16),
            pltpu.VMEM((224, 128), F32),
            pltpu.VMEM((1024, 128), F32),
            pltpu.VMEM((16, 8, 128), F32),
            pltpu.VMEM((N_EX, 16, 128), F32),
            pltpu.VMEM((N_EX, len(QUAD), 16, 128), F32),
            pltpu.SemaphoreType.DMA((A_CHUNKS,)),
            pltpu.SemaphoreType.DMA,
            pltpu.SemaphoreType.DMA((5,)),
            pltpu.SemaphoreType.DMA((2,)),
            pltpu.SemaphoreType.DMA((2,)),
            pltpu.SemaphoreType.DMA((N_EX, len(QUAD))),
            pltpu.SemaphoreType.DMA((N_EX, len(QUAD))),
        ],
        compiler_params=pltpu.CompilerParams(
            collective_id=0, has_side_effects=True, vmem_limit_bytes=48 * 1024 * 1024
        ),
        cost_estimate=pl.CostEstimate(
            flops=40_000_000, bytes_accessed=7_500_000, transcendentals=0
        ),
    )(
        *(
            pltpu.with_memory_space_constraint(value, pltpu.HBM)
            for value in (
                agg_one,
                agg_two,
                residual,
                block_cols[0],
                restrict_two,
                restrict_one[0],
                op_blocks.reshape(1024, 1728),
            )
        )
    )
    return out.reshape(1, 1024)


def solution(mesh):
    placed = (
        P("grp", "dom"),
        P("grp", "dom", None, None),
        P("grp", "dom", None),
        P("grp", None, "dom"),
        P(None, "dom"),
        P(),
        P(),
    )
    return jax.shard_map(
        body, mesh=mesh, in_specs=placed, out_specs=P("grp", "dom"), check_vma=False
    )
```

```python
from functools import partial

import jax
import jax.numpy as jnp
from jax import lax
from jax.experimental import pallas as pl
from jax.experimental.pallas import tpu as pltpu
from jax.sharding import PartitionSpec as P

S2 = 3
S3 = 4
CENTER_VALUE = 2.3
HALF_WIDTH = 1.7
F32 = jnp.float32
BF16 = jnp.bfloat16
MESH = pl.DeviceIdType.MESH
A_CHUNKS = 4
SHIFT = 2
SHIFT_FROM = 0
PAIR = ((1, 0), (1, 1), (0, 1))
QUAD = ((2, 0), (3, 0), (2, 1), (3, 1)) + PAIR
N_EX = 10


def pieces(value):
    hi = value.astype(BF16)
    lo = (value - hi.astype(F32)).astype(BF16)
    return hi, lo


def mm(a, b):
    return jnp.dot(a, b, preferred_element_type=F32)


def kernel(
    agg1_hbm,
    agg2_hbm,
    res_hbm,
    cols_hbm,
    r2_hbm,
    r1_hbm,
    a_hbm,
    out_ref,
    agg1_ref,
    agg2_ref,
    res_ref,
    cols_ref,
    r2_ref,
    a_buf,
    r1_buf,
    r31_buf,
    r2_blk,
    wp_ref,
    wr_ref,
    mask_ref,
    hot_ref,
    ug_ref,
    ax_buf,
    colsx_ref,
    hotx_ref,
    ugx_ref,
    rtx_ref,
    shift_send,
    shift_recv,
    rt_ref,
    pick_ref,
    send_buf,
    recv_buf,
    a_sem,
    r1_sem,
    in_sem,
    rx_send,
    rx_recv,
    send_sem,
    recv_sem,
):
    g = lax.axis_index("grp")
    d = lax.axis_index("dom")

    def peer(relation):
        bits, core = relation
        chip = g
        if bits & 1:
            chip = chip + 1 - 2 * (g % 2)
        if bits & 2:
            chip = chip + 2 - 4 * ((g // 2) % 2)
        return (chip, 1 - d if core else d)

    r1_copy = pltpu.make_async_copy(r1_hbm, r1_buf.at[pl.ds(d * 64, 64)], r1_sem)
    r1_copy.start()
    inputs = []
    for index, (source, target) in enumerate(
        (
            (agg1_hbm, agg1_ref),
            (agg2_hbm, agg2_ref),
            (cols_hbm, cols_ref),
            (res_hbm, res_ref),
            (r2_hbm, r2_ref),
        )
    ):
        inputs.append(pltpu.make_async_copy(source, target, in_sem.at[index]))
        inputs[-1].start()
    a_copies = []
    rows = 1024 // A_CHUNKS
    for part in range(A_CHUNKS):
        cut = pl.ds(part * rows, rows)
        a_copies.append(pltpu.make_async_copy(a_hbm.at[cut], a_buf.at[cut], a_sem.at[part]))
        a_copies[-1].start()

    barrier = pltpu.get_barrier_semaphore()
    for relation in QUAD:
        pl.semaphore_signal(barrier, inc=1, device_id=peer(relation), device_id_type=MESH)

    lane = lax.broadcasted_iota(jnp.int32, (8, 128), 1)
    row = lax.broadcasted_iota(jnp.int32, (8, 128), 0)
    left = lane < 64
    mine = (lane // 64) == d

    for copy in inputs:
        copy.wait()

    aggs = []
    for j in range(16):
        a = agg1_ref[j] // 2
        aggs.append(a)
    for jj in range(8):
        first, second = aggs[2 * jj], aggs[2 * jj + 1]
        m1 = jnp.where(left, first, second) == row
        m3 = jnp.where(left, agg2_ref[first] // 2, agg2_ref[second] // 2) == row
        cut = slice(jj * 128, (jj + 1) * 128)
        mask_ref[0, :, cut] = jnp.where(m1, 1.0, 0.0).astype(F32)
        mask_ref[1, :, cut] = jnp.where(m3, 1.0, 0.0).astype(F32)

    for j in range(16):
        pick_ref[j] = jnp.where(jnp.where(left, aggs[j], agg2_ref[aggs[j]] // 2) == row, 1.0, 0.0)

    for m in range(8):
        r2_blk[m] = r2_ref[:, m * 64 : (m + 1) * 64]

    def build_hot(columns, owner, target):
        place = columns + 16 * (owner - 1)
        valid = (place >= 0) & (place < 32)
        half = place % 2
        inner = (place // 16) * 8 + (place % 16) // 2
        even = jnp.where(valid, half * 16 + inner, -1)
        odd = jnp.where(valid, 32 + (1 - half) * 16 + inner, -1)
        spot = lax.broadcasted_iota(jnp.int32, (16, 128), 1) % 64
        for kk in range(14):
            hit = even[:, 2 * kk : 2 * kk + 1] == spot
            if 2 * kk + 1 < 27:
                hit = hit | (odd[:, 2 * kk + 1 : 2 * kk + 2] == spot)
            target[kk * 16 : (kk + 1) * 16, :] = jnp.where(hit, 1.0, 0.0).astype(BF16)

    build_hot(cols_ref[...], d, hot_ref)

    def start_sends(ex, relations, rows):
        copies = []
        for relation in relations:
            slot = QUAD.index(relation)
            copy = pltpu.make_async_remote_copy(
                src_ref=send_buf.at[ex, 0:rows],
                dst_ref=recv_buf.at[ex, slot, 0:rows],
                send_sem=send_sem.at[ex, slot],
                recv_sem=recv_sem.at[ex, slot],
                device_id=peer(relation),
                device_id_type=MESH,
            )
            copy.start()
            copies.append(copy)
        return copies

    started = []

    def own(value):
        return jnp.where(mine, value, 0.0)

    def send(ex, low, high, relations):
        send_buf[ex, 0:8] = low
        if high is not None:
            send_buf[ex, 8:16] = high
        copies = start_sends(ex, relations, 8 if high is None else 16)
        started.extend(copies)
        return copies

    def total(ex, copies, relations, base, relations_used):
        slots = [QUAD.index(relation) for relation in relations_used]
        value = send_buf[ex, base : base + 8]
        for slot in slots:
            value = value + recv_buf[ex, slot, base : base + 8]
        return value

    def restrict_part(y, group, rows):
        cut = slice(group * rows, (group + 1) * rows)
        hi1, lo1 = pieces(y * mask_ref[0, :, cut])
        hi3, lo3 = pieces(y * mask_ref[1, :, cut])
        return mm(jnp.concatenate([hi1, lo1, hi3, lo3], axis=0), wr_ref[cut])

    def restrict_end(out):
        s1 = out[0:8, 0:128] + out[8:16, 0:128]
        s3 = out[16:24, 128:256] + out[24:32, 128:256]
        return s1 + pltpu.roll(s1, 64, 1), s3 + pltpu.roll(s3, 64, 1)

    def restrict(y):
        return restrict_end(restrict_part(y, 0, 1024))

    def prolong(v, level):
        v0 = jnp.where(left, v, 0.0)
        both = jnp.concatenate([v0, v - v0], axis=0)
        hi, lo = pieces(both)
        lhs = jnp.concatenate(
            [
                jnp.concatenate([hi, hi], axis=1),
                jnp.concatenate([lo, jnp.zeros_like(lo)], axis=1),
            ],
            axis=0,
        )
        tiles = [[], []]
        for quarter in range(4):
            prod = mm(lhs, wp_ref[level, :, quarter * 256 : (quarter + 1) * 256])
            prod = prod[0:16] + prod[16:32]
            for dd in range(2):
                for part in range(2):
                    jj = 2 * quarter + part
                    tile = prod[dd * 8 : dd * 8 + 8, part * 128 : (part + 1) * 128]
                    tile = tile * mask_ref[level, :, jj * 128 : (jj + 1) * 128]
                    tile = tile + pltpu.roll(tile, 4, 0)
                    tile = tile + pltpu.roll(tile, 2, 0)
                    tile = tile + pltpu.roll(tile, 1, 0)
                    tiles[dd].append(tile)
        return tiles

    def rows_of(tiles):
        value = tiles[0]
        for jj in range(1, 8):
            value = jnp.where(row == jj, tiles[jj], value)
        return value

    def own_rows(tiles):
        return jnp.where(d == 0, rows_of(tiles[0]), rows_of(tiles[1]))

    def apply(v, level, shifted=True):
        tiles = prolong(v, level)
        u = jnp.concatenate([rows_of(tiles[0]), rows_of(tiles[1])], axis=0)
        turned = pltpu.roll(u, 64, 1)
        left16 = jnp.concatenate([left, left], axis=0)
        spread = jnp.concatenate(
            [
                jnp.where(left16, u, 0.0),
                jnp.where(left16, turned, 0.0),
                jnp.where(left16, 0.0, u),
                jnp.where(left16, 0.0, turned),
            ],
            axis=0,
        )
        hi, lo = pieces(spread)
        rhs = jnp.concatenate([hi, lo], axis=0)
        ug_ref[...] = mm(hot_ref[...], rhs)

        def blocks(numbers, a_ref, u_ref, r_ref, first):
            out = None
            for i in numbers:
                base = (i - first) * 64
                acc = jnp.zeros((8, 8, 128), F32)
                for kk in range(13):
                    u = jnp.broadcast_to(u_ref[kk * 16 + i : kk * 16 + i + 1, :], (8, 128))
                    block = a_ref[base : base + 64, kk * 128 : (kk + 1) * 128]
                    acc = acc + block.reshape(8, 8, 128) * u[None]
                u = jnp.broadcast_to(u_ref[13 * 16 + i : 13 * 16 + i + 1, :], (8, 128))
                tail = a_ref[base : base + 64, 1664:1728].reshape(8, 8, 64) * u[None, :, 0:64]
                acc = acc + jnp.concatenate([tail, jnp.zeros((8, 8, 64), F32)], axis=2)
                y = jnp.sum(acc.reshape(64, 128), axis=1, keepdims=True)
                part = jnp.sum((r_ref[base : base + 64, :] * y).reshape(8, 8, 128), axis=0)
                part = part + pltpu.roll(part, 4, 0)
                part = part + pltpu.roll(part, 2, 0)
                part = (part + pltpu.roll(part, 1, 0)) * pick_ref[i]
                out = part if out is None else out + part
            return out

        if shifted:
            out = blocks(range(16 - SHIFT), a_buf, ug_ref, rt_ref, 0)
            last = range(16 - SHIFT, 16)

            def both_ends():
                ugx_ref[...] = mm(hotx_ref[...], rhs)
                return (
                    blocks(last, a_buf, ug_ref, rt_ref, 0),
                    blocks(last, ax_buf, ugx_ref, rtx_ref, 16 - SHIFT),
                )

            def neither():
                return jnp.zeros((8, 128), F32), jnp.zeros((8, 128), F32)

            more, other = lax.cond(d == 1, both_ends, neither)
            out = out + more
        else:
            out = blocks(range(16), a_buf, ug_ref, rt_ref, 0)
            other = jnp.zeros((8, 128), F32)
        turned = pltpu.roll(out, 64, 1)
        other_turned = pltpu.roll(other, 64, 1)
        w = jnp.where(mine, jnp.where(left, out, turned), jnp.where(left, other, other_turned))
        w3 = jnp.where(mine, jnp.where(left, turned, out), jnp.where(left, other_turned, other))
        return w, w3

    r1_copy.wait()
    own_r1 = r1_buf[pl.ds(pl.multiple_of(d * 64, 64), 64), :]
    hi, lo = pieces(own_r1.T)
    rt_ref[:, 0:64] = own_r1.T
    wr_ref[:, 0:64] = hi
    wr_ref[:, 64:128] = lo
    wr_ref[:, 128:256] = jnp.zeros((1024, 128), BF16)

    pl.semaphore_wait(barrier, len(QUAD))

    def swap_copy(buf, index):
        ref = buf.at[pl.ds(d * 64, 64)]
        return pltpu.make_async_remote_copy(
            src_ref=ref,
            dst_ref=ref,
            send_sem=rx_send.at[index],
            recv_sem=rx_recv.at[index],
            device_id=(g, 1 - d),
            device_id_type=MESH,
        )

    swap1 = swap_copy(r1_buf, 0)
    swap1.start()
    cols_copy = pltpu.make_async_remote_copy(
        src_ref=cols_ref,
        dst_ref=colsx_ref,
        send_sem=shift_send.at[0],
        recv_sem=shift_recv.at[0],
        device_id=(g, 1 - d),
        device_id_type=MESH,
    )
    cols_copy.start()

    y0 = jnp.broadcast_to(res_ref[...], (8, 1024))
    w, unused = restrict(y0)
    copies = send(0, own(w), None, PAIR)

    a_copy = pltpu.make_async_remote_copy(
        src_ref=a_hbm.at[pl.ds(64 * (16 - SHIFT), 64 * SHIFT)],
        dst_ref=ax_buf,
        send_sem=shift_send.at[1],
        recv_sem=shift_recv.at[1],
        device_id=(g, 1 - d),
        device_id_type=MESH,
    )

    @pl.when(d == 0)
    def _():
        a_copy.start()

    for jj in range(8):
        parts = []
        for half_at in range(2):
            j = 2 * jj + half_at
            parts.append(
                jnp.dot(
                    r2_blk[aggs[j]],
                    own_r1[:, j * 64 : (j + 1) * 64],
                    preferred_element_type=F32,
                    precision=lax.Precision.HIGHEST,
                )
            )
        r31_buf[pl.ds(pl.multiple_of(d * 64, 64), 64), jj * 128 : (jj + 1) * 128] = jnp.concatenate(
            parts, axis=1
        )
    own_r31 = r31_buf[pl.ds(pl.multiple_of(d * 64, 64), 64), :]
    swap3 = swap_copy(r31_buf, 1)
    swap3.start()
    hi, lo = pieces(own_r31.T)
    rt_ref[:, 64:128] = own_r31.T
    wr_ref[:, 128:192] = hi
    wr_ref[:, 192:256] = lo
    unused, coarse = restrict(y0)
    coarse = own(coarse)

    swap1.wait()
    hi, lo = pieces(r1_buf[...])
    wp_ref[0, 0:128] = hi
    wp_ref[0, 128:256] = lo

    cols_copy.wait()
    build_hot(colsx_ref[...], 1 - d, hotx_ref)
    rtx_ref[:, 0:64] = r1_buf[pl.ds(pl.multiple_of((1 - d) * 64, 64), 64), 64 * (16 - SHIFT) :].T
    swap3.wait()
    rtx_ref[:, 64:128] = r31_buf[pl.ds(pl.multiple_of((1 - d) * 64, 64), 64), 64 * (16 - SHIFT) :].T
    hi, lo = pieces(r31_buf[...])
    wp_ref[1, 0:128] = hi
    wp_ref[1, 128:256] = lo
    for copy in a_copies:
        copy.wait()

    spread_ratio = CENTER_VALUE / HALF_WIDTH

    def wait_all(copies):
        for copy in copies:
            copy.wait_recv()

    def pair_total(ex, copies):
        wait_all(copies)
        return total(ex, copies, PAIR, 0, PAIR)

    def quad_total(ex, copies, base=0):
        wait_all(copies)
        return total(ex, copies, QUAD, base, QUAD)

    rest = pair_total(0, copies)
    start = jnp.zeros((8, 128), F32)
    direction = rest / CENTER_VALUE
    ratio = 1.0 / spread_ratio
    for sweep in range(S2):
        ex = 1 + sweep
        start = start + direction
        if sweep == SHIFT_FROM:

            @pl.when(d == 1)
            def _():
                a_copy.wait_recv()

        w, w3 = apply(direction, 0, sweep >= SHIFT_FROM)
        coarse = coarse - w3
        if sweep == S2 - 1:
            copies = send(ex, w, coarse, QUAD)
            wait_all(copies)
            rest = rest - total(ex, copies, QUAD, 0, PAIR)
            rhs3 = total(ex, copies, QUAD, 8, QUAD)
        else:
            copies = send(ex, w, None, PAIR)
            rest = rest - pair_total(ex, copies)
            ratio_next = 1.0 / (2.0 * spread_ratio - ratio)
            direction = ratio_next * ratio * direction + 2.0 * ratio_next / HALF_WIDTH * rest
            ratio = ratio_next

    rest3 = rhs3
    coarse_sol = jnp.zeros((8, 128), F32)
    direction = rest3 / CENTER_VALUE
    ratio = 1.0 / spread_ratio
    for sweep in range(S3):
        coarse_sol = coarse_sol + direction
        if sweep < S3 - 1:
            ex = 1 + S2 + sweep
            unused, w3 = apply(direction, 1)
            copies = send(ex, w3, None, QUAD)
            rest3 = rest3 - quad_total(ex, copies)
            ratio_next = 1.0 / (2.0 * spread_ratio - ratio)
            direction = ratio_next * ratio * direction + 2.0 * ratio_next / HALF_WIDTH * rest3
            ratio = ratio_next

    ex = S2 + S3
    w, unused = apply(coarse_sol, 1)
    copies = send(ex, w, None, PAIR)
    fine_coarse = own_rows(prolong(coarse_sol, 1))
    rest = rest - pair_total(ex, copies)
    direction = rest / CENTER_VALUE
    ratio = 1.0 / spread_ratio
    for sweep in range(S2):
        start = start + direction
        if sweep < S2 - 1:
            ex = S2 + S3 + 1 + sweep
            w, unused = apply(direction, 0)
            copies = send(ex, w, None, PAIR)
            rest = rest - pair_total(ex, copies)
            ratio_next = 1.0 / (2.0 * spread_ratio - ratio)
            direction = ratio_next * ratio * direction + 2.0 * ratio_next / HALF_WIDTH * rest
            ratio = ratio_next

    out_ref[...] = own_rows(prolong(start, 0)) + fine_coarse

    for copy in started:
        copy.wait_send()

    @pl.when(d == 0)
    def _():
        a_copy.wait_send()


def body(residual, op_blocks, block_cols, restrict_one, restrict_two, agg_one, agg_two):
    vmem = pl.BlockSpec(memory_space=pltpu.VMEM)
    hbm = pl.BlockSpec(memory_space=pltpu.HBM)
    out = pl.pallas_call(
        kernel,
        out_shape=jax.ShapeDtypeStruct((8, 128), F32),
        in_specs=[hbm] * 7,
        out_specs=vmem,
        scratch_shapes=[
            pltpu.SMEM((16,), jnp.int32),
            pltpu.SMEM((8,), jnp.int32),
            pltpu.VMEM((1, 1024), F32),
            pltpu.VMEM((16, 27), jnp.int32),
            pltpu.VMEM((64, 512), F32),
            pltpu.VMEM((1024, 1728), F32),
            pltpu.VMEM((128, 1024), F32),
            pltpu.VMEM((128, 1024), F32),
            pltpu.VMEM((8, 64, 64), F32),
            pltpu.VMEM((2, 256, 1024), BF16),
            pltpu.VMEM((1024, 256), BF16),
            pltpu.VMEM((2, 8, 1024), F32),
            pltpu.VMEM((224, 128), BF16),
            pltpu.VMEM((224, 128), F32),
            pltpu.VMEM((64 * SHIFT, 1728), F32),
            pltpu.VMEM((16, 27), jnp.int32),
            pltpu.VMEM((224, 128), BF16),
            pltpu.VMEM((224, 128), F32),
            pltpu.VMEM((64 * SHIFT, 128), F32),
            pltpu.SemaphoreType.DMA((2,)),
            pltpu.SemaphoreType.DMA((2,)),
            pltpu.VMEM((1024, 128), F32),
            pltpu.VMEM((16, 8, 128), F32),
            pltpu.VMEM((N_EX, 16, 128), F32),
            pltpu.VMEM((N_EX, len(QUAD), 16, 128), F32),
            pltpu.SemaphoreType.DMA((A_CHUNKS,)),
            pltpu.SemaphoreType.DMA,
            pltpu.SemaphoreType.DMA((5,)),
            pltpu.SemaphoreType.DMA((2,)),
            pltpu.SemaphoreType.DMA((2,)),
            pltpu.SemaphoreType.DMA((N_EX, len(QUAD))),
            pltpu.SemaphoreType.DMA((N_EX, len(QUAD))),
        ],
        compiler_params=pltpu.CompilerParams(
            collective_id=0, has_side_effects=True, vmem_limit_bytes=48 * 1024 * 1024
        ),
        cost_estimate=pl.CostEstimate(
            flops=40_000_000, bytes_accessed=7_500_000, transcendentals=0
        ),
    )(
        *(
            pltpu.with_memory_space_constraint(value, pltpu.HBM)
            for value in (
                agg_one,
                agg_two,
                residual,
                block_cols[0],
                restrict_two,
                restrict_one[0],
                op_blocks.reshape(1024, 1728),
            )
        )
    )
    return out.reshape(1, 1024)


def solution(mesh):
    placed = (
        P("grp", "dom"),
        P("grp", "dom", None, None),
        P("grp", "dom", None),
        P("grp", None, "dom"),
        P(None, "dom"),
        P(),
        P(),
    )
    return jax.shard_map(
        body, mesh=mesh, in_specs=placed, out_specs=P("grp", "dom"), check_vma=False
    )
```

```python
from functools import partial

import jax
import jax.numpy as jnp
from jax import lax
from jax.experimental import pallas as pl
from jax.experimental.pallas import tpu as pltpu
from jax.sharding import PartitionSpec as P

S2 = 3
S3 = 4
CENTER_VALUE = 2.3
HALF_WIDTH = 1.7
F32 = jnp.float32
BF16 = jnp.bfloat16
MESH = pl.DeviceIdType.MESH
A_CHUNKS = 4
SHIFT = 2
SHIFT_FROM = 0
PAIR = ((1, 0), (1, 1), (0, 1))
QUAD = ((2, 0), (3, 0), (2, 1), (3, 1)) + PAIR
N_EX = 10


def pieces(value):
    hi = value.astype(BF16)
    lo = (value - hi.astype(F32)).astype(BF16)
    return hi, lo


def mm(a, b):
    return jnp.dot(a, b, preferred_element_type=F32)


def kernel(
    agg1_hbm,
    agg2_hbm,
    res_hbm,
    cols_hbm,
    r2_hbm,
    r1_hbm,
    a_hbm,
    out_ref,
    agg1_ref,
    agg2_ref,
    res_ref,
    cols_ref,
    r2_ref,
    a_buf,
    r1_buf,
    r31_buf,
    r2_blk,
    wp_ref,
    wr_ref,
    mask_ref,
    hot_ref,
    ug_ref,
    ax_buf,
    colsx_ref,
    hotx_ref,
    ugx_ref,
    rtx_ref,
    shift_send,
    shift_recv,
    rt_ref,
    pick_ref,
    send_buf,
    recv_buf,
    a_sem,
    r1_sem,
    in_sem,
    rx_send,
    rx_recv,
    send_sem,
    recv_sem,
):
    g = lax.axis_index("grp")
    d = lax.axis_index("dom")

    def peer(relation):
        bits, core = relation
        chip = g
        if bits & 1:
            chip = chip + 1 - 2 * (g % 2)
        if bits & 2:
            chip = chip + 2 - 4 * ((g // 2) % 2)
        return (chip, 1 - d if core else d)

    barrier = pltpu.get_barrier_semaphore()
    for relation in QUAD:
        pl.semaphore_signal(barrier, inc=1, device_id=peer(relation), device_id_type=MESH)

    r1_copy = pltpu.make_async_copy(r1_hbm, r1_buf.at[pl.ds(d * 64, 64)], r1_sem)
    r1_copy.start()
    inputs = []
    for index, (source, target) in enumerate(
        (
            (agg1_hbm, agg1_ref),
            (agg2_hbm, agg2_ref),
            (res_hbm, res_ref),
            (cols_hbm, cols_ref),
            (r2_hbm, r2_ref),
        )
    ):
        inputs.append(pltpu.make_async_copy(source, target, in_sem.at[index]))
        inputs[-1].start()
    a_copies = []
    rows = 1024 // A_CHUNKS
    for part in range(A_CHUNKS):
        cut = pl.ds(part * rows, rows)
        a_copies.append(pltpu.make_async_copy(a_hbm.at[cut], a_buf.at[cut], a_sem.at[part]))
        a_copies[-1].start()

    lane = lax.broadcasted_iota(jnp.int32, (8, 128), 1)
    row = lax.broadcasted_iota(jnp.int32, (8, 128), 0)
    left = lane < 64
    mine = (lane // 64) == d

    for copy in inputs[0:3]:
        copy.wait()

    aggs = []
    for j in range(16):
        a = agg1_ref[j] // 2
        aggs.append(a)
    for jj in range(8):
        first, second = aggs[2 * jj], aggs[2 * jj + 1]
        m1 = jnp.where(left, first, second) == row
        m3 = jnp.where(left, agg2_ref[first] // 2, agg2_ref[second] // 2) == row
        cut = slice(jj * 128, (jj + 1) * 128)
        mask_ref[0, :, cut] = jnp.where(m1, 1.0, 0.0).astype(F32)
        mask_ref[1, :, cut] = jnp.where(m3, 1.0, 0.0).astype(F32)

    def build_hot(columns, owner, target):
        place = columns + 16 * (owner - 1)
        valid = (place >= 0) & (place < 32)
        half = place % 2
        inner = (place // 16) * 8 + (place % 16) // 2
        even = jnp.where(valid, half * 16 + inner, -1)
        odd = jnp.where(valid, 32 + (1 - half) * 16 + inner, -1)
        spot = lax.broadcasted_iota(jnp.int32, (16, 128), 1) % 64
        for kk in range(14):
            hit = even[:, 2 * kk : 2 * kk + 1] == spot
            if 2 * kk + 1 < 27:
                hit = hit | (odd[:, 2 * kk + 1 : 2 * kk + 2] == spot)
            target[kk * 16 : (kk + 1) * 16, :] = jnp.where(hit, 1.0, 0.0).astype(BF16)

    def start_sends(ex, relations, rows):
        copies = []
        for relation in relations:
            slot = QUAD.index(relation)
            copy = pltpu.make_async_remote_copy(
                src_ref=send_buf.at[ex, 0:rows],
                dst_ref=recv_buf.at[ex, slot, 0:rows],
                send_sem=send_sem.at[ex, slot],
                recv_sem=recv_sem.at[ex, slot],
                device_id=peer(relation),
                device_id_type=MESH,
            )
            copy.start()
            copies.append(copy)
        return copies

    started = []

    def own(value):
        return jnp.where(mine, value, 0.0)

    def send(ex, low, high, relations, rows=8):
        send_buf[ex, 0:8] = low
        if high is not None:
            send_buf[ex, 8:16] = high
        copies = start_sends(ex, relations, rows)
        started.extend(copies)
        return copies

    def total(ex, relations, base, rows):
        value = send_buf[ex, base : base + rows]
        for relation in relations:
            value = value + recv_buf[ex, QUAD.index(relation), base : base + rows]
        if rows < 8:
            value = jnp.concatenate([value, jnp.zeros((8 - rows, 128), F32)], axis=0)
        return value

    def restrict_part(y, group, rows):
        cut = slice(group * rows, (group + 1) * rows)
        hi1, lo1 = pieces(y * mask_ref[0, :, cut])
        hi3, lo3 = pieces(y * mask_ref[1, :, cut])
        return mm(jnp.concatenate([hi1, lo1, hi3, lo3], axis=0), wr_ref[cut])

    def restrict_end(out):
        s1 = out[0:8, 0:128] + out[8:16, 0:128]
        s3 = out[16:24, 128:256] + out[24:32, 128:256]
        return s1 + pltpu.roll(s1, 64, 1), s3 + pltpu.roll(s3, 64, 1)

    def restrict(y):
        return restrict_end(restrict_part(y, 0, 1024))

    def prolong(v, level):
        v0 = jnp.where(left, v, 0.0)
        both = jnp.concatenate([v0, v - v0], axis=0)
        hi, lo = pieces(both)
        lhs = jnp.concatenate(
            [
                jnp.concatenate([hi, hi], axis=1),
                jnp.concatenate([lo, jnp.zeros_like(lo)], axis=1),
            ],
            axis=0,
        )
        tiles = [[], []]
        for quarter in range(4):
            prod = mm(lhs, wp_ref[level, :, quarter * 256 : (quarter + 1) * 256])
            prod = prod[0:16] + prod[16:32]
            for dd in range(2):
                for part in range(2):
                    jj = 2 * quarter + part
                    tile = prod[dd * 8 : dd * 8 + 8, part * 128 : (part + 1) * 128]
                    tile = tile * mask_ref[level, :, jj * 128 : (jj + 1) * 128]
                    tile = tile + pltpu.roll(tile, 4, 0)
                    tile = tile + pltpu.roll(tile, 2, 0)
                    tile = tile + pltpu.roll(tile, 1, 0)
                    tiles[dd].append(tile)
        return tiles

    def rows_of(tiles):
        value = tiles[0]
        for jj in range(1, 8):
            value = jnp.where(row == jj, tiles[jj], value)
        return value

    def own_rows(tiles):
        return jnp.where(d == 0, rows_of(tiles[0]), rows_of(tiles[1]))

    def apply(v, level, shifted=True):
        tiles = prolong(v, level)
        u = jnp.concatenate([rows_of(tiles[0]), rows_of(tiles[1])], axis=0)
        turned = pltpu.roll(u, 64, 1)
        left16 = jnp.concatenate([left, left], axis=0)
        spread = jnp.concatenate(
            [
                jnp.where(left16, u, 0.0),
                jnp.where(left16, turned, 0.0),
                jnp.where(left16, 0.0, u),
                jnp.where(left16, 0.0, turned),
            ],
            axis=0,
        )
        hi, lo = pieces(spread)
        rhs = jnp.concatenate([hi, lo], axis=0)
        ug_ref[...] = mm(hot_ref[...], rhs)

        def blocks(numbers, a_ref, u_ref, r_ref, first):
            out = None
            for i in numbers:
                base = (i - first) * 64
                acc = jnp.zeros((8, 8, 128), F32)
                for kk in range(13):
                    u = jnp.broadcast_to(u_ref[kk * 16 + i : kk * 16 + i + 1, :], (8, 128))
                    block = a_ref[base : base + 64, kk * 128 : (kk + 1) * 128]
                    acc = acc + block.reshape(8, 8, 128) * u[None]
                u = jnp.broadcast_to(u_ref[13 * 16 + i : 13 * 16 + i + 1, :], (8, 128))
                tail = a_ref[base : base + 64, 1664:1728].reshape(8, 8, 64) * u[None, :, 0:64]
                acc = acc + jnp.concatenate([tail, jnp.zeros((8, 8, 64), F32)], axis=2)
                y = jnp.sum(acc.reshape(64, 128), axis=1, keepdims=True)
                part = jnp.sum((r_ref[base : base + 64, :] * y).reshape(8, 8, 128), axis=0)
                part = part + pltpu.roll(part, 4, 0)
                part = part + pltpu.roll(part, 2, 0)
                part = (part + pltpu.roll(part, 1, 0)) * pick_ref[i]
                out = part if out is None else out + part
            return out

        if shifted:
            out = blocks(range(16 - SHIFT), a_buf, ug_ref, rt_ref, 0)
            last = range(16 - SHIFT, 16)

            def both_ends():
                ugx_ref[...] = mm(hotx_ref[...], rhs)
                return (
                    blocks(last, a_buf, ug_ref, rt_ref, 0),
                    blocks(last, ax_buf, ugx_ref, rtx_ref, 16 - SHIFT),
                )

            def neither():
                return jnp.zeros((8, 128), F32), jnp.zeros((8, 128), F32)

            more, other = lax.cond(d == 1, both_ends, neither)
            out = out + more
        else:
            out = blocks(range(16), a_buf, ug_ref, rt_ref, 0)
            other = jnp.zeros((8, 128), F32)
        turned = pltpu.roll(out, 64, 1)
        other_turned = pltpu.roll(other, 64, 1)
        w = jnp.where(mine, jnp.where(left, out, turned), jnp.where(left, other, other_turned))
        w3 = jnp.where(mine, jnp.where(left, turned, out), jnp.where(left, other_turned, other))
        return w, w3

    r1_copy.wait()
    own_r1 = r1_buf[pl.ds(pl.multiple_of(d * 64, 64), 64), :]
    hi, lo = pieces(own_r1.T)
    wr_ref[:, 0:64] = hi
    wr_ref[:, 64:128] = lo

    pl.semaphore_wait(barrier, len(QUAD))

    def swap_copy(buf, index):
        ref = buf.at[pl.ds(d * 64, 64)]
        return pltpu.make_async_remote_copy(
            src_ref=ref,
            dst_ref=ref,
            send_sem=rx_send.at[index],
            recv_sem=rx_recv.at[index],
            device_id=(g, 1 - d),
            device_id_type=MESH,
        )

    swap1 = swap_copy(r1_buf, 0)
    swap1.start()
    y0 = jnp.broadcast_to(res_ref[...], (8, 1024))
    hi, lo = pieces(y0 * mask_ref[0])
    w = mm(jnp.concatenate([hi, lo], axis=0), wr_ref[:, 0:128])
    w = w[0:8] + w[8:16]
    w = w + pltpu.roll(w, 64, 1)
    copies = send(0, own(w), None, PAIR)

    for copy in inputs[3:5]:
        copy.wait()
    cols_copy = pltpu.make_async_remote_copy(
        src_ref=cols_ref,
        dst_ref=colsx_ref,
        send_sem=shift_send.at[0],
        recv_sem=shift_recv.at[0],
        device_id=(g, 1 - d),
        device_id_type=MESH,
    )
    cols_copy.start()

    a_copy = pltpu.make_async_remote_copy(
        src_ref=a_hbm.at[pl.ds(64 * (16 - SHIFT), 64 * SHIFT)],
        dst_ref=ax_buf,
        send_sem=shift_send.at[1],
        recv_sem=shift_recv.at[1],
        device_id=(g, 1 - d),
        device_id_type=MESH,
    )

    @pl.when(d == 0)
    def _():
        a_copy.start()

    for m in range(8):
        r2_blk[m] = r2_ref[:, m * 64 : (m + 1) * 64]

    for jj in range(8):
        parts = []
        for half_at in range(2):
            j = 2 * jj + half_at
            parts.append(
                jnp.dot(
                    r2_blk[aggs[j]],
                    own_r1[:, j * 64 : (j + 1) * 64],
                    preferred_element_type=F32,
                    precision=lax.Precision.HIGHEST,
                )
            )
        r31_buf[pl.ds(pl.multiple_of(d * 64, 64), 64), jj * 128 : (jj + 1) * 128] = jnp.concatenate(
            parts, axis=1
        )
    own_r31 = r31_buf[pl.ds(pl.multiple_of(d * 64, 64), 64), :]
    swap3 = swap_copy(r31_buf, 1)
    swap3.start()
    hi, lo = pieces(own_r31.T)
    rt_ref[:, 64:128] = own_r31.T
    wr_ref[:, 128:192] = hi
    wr_ref[:, 192:256] = lo
    unused, coarse = restrict(y0)
    coarse = own(coarse)

    swap1.wait()
    hi, lo = pieces(r1_buf[...])
    wp_ref[0, 0:128] = hi
    wp_ref[0, 128:256] = lo

    for j in range(16):
        pick_ref[j] = jnp.where(jnp.where(left, aggs[j], agg2_ref[aggs[j]] // 2) == row, 1.0, 0.0)

    rt_ref[:, 0:64] = own_r1.T
    build_hot(cols_ref[...], d, hot_ref)
    cols_copy.wait()
    build_hot(colsx_ref[...], 1 - d, hotx_ref)
    rtx_ref[:, 0:64] = r1_buf[pl.ds(pl.multiple_of((1 - d) * 64, 64), 64), 64 * (16 - SHIFT) :].T
    swap3.wait()
    rtx_ref[:, 64:128] = r31_buf[pl.ds(pl.multiple_of((1 - d) * 64, 64), 64), 64 * (16 - SHIFT) :].T
    for copy in a_copies:
        copy.wait()

    spread_ratio = CENTER_VALUE / HALF_WIDTH

    def wait_all(copies):
        for copy in copies:
            copy.wait_recv()

    def pair_total(ex, copies):
        wait_all(copies)
        return total(ex, PAIR, 0, 8)

    def quad_total(ex, copies):
        wait_all(copies)
        return total(ex, QUAD, 0, 4)

    rest = pair_total(0, copies)
    start = jnp.zeros((8, 128), F32)
    direction = rest / CENTER_VALUE
    ratio = 1.0 / spread_ratio
    for sweep in range(S2):
        ex = 1 + sweep
        start = start + direction
        if sweep == SHIFT_FROM:

            @pl.when(d == 1)
            def _():
                a_copy.wait_recv()

        w, w3 = apply(direction, 0, sweep >= SHIFT_FROM)
        coarse = coarse - w3
        if sweep == S2 - 1:
            copies = send(ex, w, coarse, QUAD, 12)
            wait_all(copies)
            rest = rest - total(ex, PAIR, 0, 8)
            rhs3 = total(ex, QUAD, 8, 4)
        else:
            copies = send(ex, w, None, PAIR)
            if sweep == 0:
                hi, lo = pieces(r31_buf[...])
                wp_ref[1, 0:128] = hi
                wp_ref[1, 128:256] = lo
            rest = rest - pair_total(ex, copies)
            ratio_next = 1.0 / (2.0 * spread_ratio - ratio)
            direction = ratio_next * ratio * direction + 2.0 * ratio_next / HALF_WIDTH * rest
            ratio = ratio_next

    rest3 = rhs3
    coarse_sol = jnp.zeros((8, 128), F32)
    direction = rest3 / CENTER_VALUE
    ratio = 1.0 / spread_ratio
    for sweep in range(S3):
        coarse_sol = coarse_sol + direction
        if sweep < S3 - 1:
            ex = 1 + S2 + sweep
            unused, w3 = apply(direction, 1)
            copies = send(ex, w3, None, QUAD, 4)
            rest3 = rest3 - quad_total(ex, copies)
            ratio_next = 1.0 / (2.0 * spread_ratio - ratio)
            direction = ratio_next * ratio * direction + 2.0 * ratio_next / HALF_WIDTH * rest3
            ratio = ratio_next

    ex = S2 + S3
    w, unused = apply(coarse_sol, 1)
    copies = send(ex, w, None, PAIR)
    fine_coarse = own_rows(prolong(coarse_sol, 1))
    rest = rest - pair_total(ex, copies)
    direction = rest / CENTER_VALUE
    ratio = 1.0 / spread_ratio
    for sweep in range(S2):
        start = start + direction
        if sweep < S2 - 1:
            ex = S2 + S3 + 1 + sweep
            w, unused = apply(direction, 0)
            copies = send(ex, w, None, PAIR)
            rest = rest - pair_total(ex, copies)
            ratio_next = 1.0 / (2.0 * spread_ratio - ratio)
            direction = ratio_next * ratio * direction + 2.0 * ratio_next / HALF_WIDTH * rest
            ratio = ratio_next

    out_ref[...] = own_rows(prolong(start, 0)) + fine_coarse

    for copy in started:
        copy.wait_send()

    @pl.when(d == 0)
    def _():
        a_copy.wait_send()


def body(residual, op_blocks, block_cols, restrict_one, restrict_two, agg_one, agg_two):
    vmem = pl.BlockSpec(memory_space=pltpu.VMEM)
    hbm = pl.BlockSpec(memory_space=pltpu.HBM)
    out = pl.pallas_call(
        kernel,
        out_shape=jax.ShapeDtypeStruct((8, 128), F32),
        in_specs=[hbm] * 7,
        out_specs=vmem,
        scratch_shapes=[
            pltpu.SMEM((16,), jnp.int32),
            pltpu.SMEM((8,), jnp.int32),
            pltpu.VMEM((1, 1024), F32),
            pltpu.VMEM((16, 27), jnp.int32),
            pltpu.VMEM((64, 512), F32),
            pltpu.VMEM((1024, 1728), F32),
            pltpu.VMEM((128, 1024), F32),
            pltpu.VMEM((128, 1024), F32),
            pltpu.VMEM((8, 64, 64), F32),
            pltpu.VMEM((2, 256, 1024), BF16),
            pltpu.VMEM((1024, 256), BF16),
            pltpu.VMEM((2, 8, 1024), F32),
            pltpu.VMEM((224, 128), BF16),
            pltpu.VMEM((224, 128), F32),
            pltpu.VMEM((64 * SHIFT, 1728), F32),
            pltpu.VMEM((16, 27), jnp.int32),
            pltpu.VMEM((224, 128), BF16),
            pltpu.VMEM((224, 128), F32),
            pltpu.VMEM((64 * SHIFT, 128), F32),
            pltpu.SemaphoreType.DMA((2,)),
            pltpu.SemaphoreType.DMA((2,)),
            pltpu.VMEM((1024, 128), F32),
            pltpu.VMEM((16, 8, 128), F32),
            pltpu.VMEM((N_EX, 16, 128), F32),
            pltpu.VMEM((N_EX, len(QUAD), 16, 128), F32),
            pltpu.SemaphoreType.DMA((A_CHUNKS,)),
            pltpu.SemaphoreType.DMA,
            pltpu.SemaphoreType.DMA((5,)),
            pltpu.SemaphoreType.DMA((2,)),
            pltpu.SemaphoreType.DMA((2,)),
            pltpu.SemaphoreType.DMA((N_EX, len(QUAD))),
            pltpu.SemaphoreType.DMA((N_EX, len(QUAD))),
        ],
        compiler_params=pltpu.CompilerParams(
            collective_id=0, has_side_effects=True, vmem_limit_bytes=48 * 1024 * 1024
        ),
        cost_estimate=pl.CostEstimate(
            flops=40_000_000, bytes_accessed=7_500_000, transcendentals=0
        ),
    )(
        *(
            pltpu.with_memory_space_constraint(value, pltpu.HBM)
            for value in (
                agg_one,
                agg_two,
                residual,
                block_cols[0],
                restrict_two,
                restrict_one[0],
                op_blocks.reshape(1024, 1728),
            )
        )
    )
    return out.reshape(1, 1024)


def solution(mesh):
    placed = (
        P("grp", "dom"),
        P("grp", "dom", None, None),
        P("grp", "dom", None),
        P("grp", None, "dom"),
        P(None, "dom"),
        P(),
        P(),
    )
    return jax.shard_map(
        body, mesh=mesh, in_specs=placed, out_specs=P("grp", "dom"), check_vma=False
    )
```

```python
from functools import partial

import jax
import jax.numpy as jnp
from jax import lax
from jax.experimental import pallas as pl
from jax.experimental.pallas import tpu as pltpu
from jax.sharding import PartitionSpec as P

S2 = 3
S3 = 4
CENTER_VALUE = 2.3
HALF_WIDTH = 1.7
F32 = jnp.float32
BF16 = jnp.bfloat16
MESH = pl.DeviceIdType.MESH
A_CHUNKS = 1
SHIFT = 2
SHIFT_FROM = 0
PAIR = ((1, 0), (1, 1), (0, 1))
QUAD = ((2, 0), (3, 0), (2, 1), (3, 1)) + PAIR
N_EX = 10


def pieces(value):
    hi = value.astype(BF16)
    lo = (value - hi.astype(F32)).astype(BF16)
    return hi, lo


def mm(a, b):
    return jnp.dot(a, b, preferred_element_type=F32)


def kernel(
    agg1_hbm,
    agg2_hbm,
    res_hbm,
    cols_hbm,
    r2_hbm,
    r1_hbm,
    a_hbm,
    out_ref,
    agg1_ref,
    agg2_ref,
    res_ref,
    cols_ref,
    r2_ref,
    a_buf,
    r1_buf,
    r31_buf,
    r2_blk,
    wp_ref,
    wr_ref,
    mask_ref,
    hot_ref,
    ug_ref,
    ax_buf,
    colsx_ref,
    hotx_ref,
    ugx_ref,
    rtx_ref,
    shift_send,
    shift_recv,
    rt_ref,
    pick_ref,
    send_buf,
    recv_buf,
    a_sem,
    r1_sem,
    in_sem,
    rx_send,
    rx_recv,
    send_sem,
    recv_sem,
):
    g = lax.axis_index("grp")
    d = lax.axis_index("dom")

    def peer(relation):
        bits, core = relation
        chip = g
        if bits & 1:
            chip = chip + 1 - 2 * (g % 2)
        if bits & 2:
            chip = chip + 2 - 4 * ((g // 2) % 2)
        return (chip, 1 - d if core else d)

    barrier = pltpu.get_barrier_semaphore()
    for relation in QUAD:
        pl.semaphore_signal(barrier, inc=1, device_id=peer(relation), device_id_type=MESH)

    r1_copy = pltpu.make_async_copy(r1_hbm, r1_buf.at[pl.ds(d * 64, 64)], r1_sem)
    r1_copy.start()
    inputs = []
    for index, (source, target) in enumerate(
        (
            (agg1_hbm, agg1_ref),
            (agg2_hbm, agg2_ref),
            (res_hbm, res_ref),
            (cols_hbm, cols_ref),
            (r2_hbm, r2_ref),
        )
    ):
        inputs.append(pltpu.make_async_copy(source, target, in_sem.at[index]))
        inputs[-1].start()
    a_copies = []
    rows = 1024 // A_CHUNKS
    for part in range(A_CHUNKS):
        cut = pl.ds(part * rows, rows)
        a_copies.append(pltpu.make_async_copy(a_hbm.at[cut], a_buf.at[cut], a_sem.at[part]))
        a_copies[-1].start()

    lane = lax.broadcasted_iota(jnp.int32, (8, 128), 1)
    row = lax.broadcasted_iota(jnp.int32, (8, 128), 0)
    left = lane < 64
    mine = (lane // 64) == d

    for copy in inputs[0:3]:
        copy.wait()

    aggs = []
    for j in range(16):
        a = agg1_ref[j] // 2
        aggs.append(a)
    for jj in range(8):
        first, second = aggs[2 * jj], aggs[2 * jj + 1]
        m1 = jnp.where(left, first, second) == row
        m3 = jnp.where(left, agg2_ref[first] // 2, agg2_ref[second] // 2) == row
        cut = slice(jj * 128, (jj + 1) * 128)
        mask_ref[0, :, cut] = jnp.where(m1, 1.0, 0.0).astype(F32)
        mask_ref[1, :, cut] = jnp.where(m3, 1.0, 0.0).astype(F32)

    def build_hot(columns, owner, target):
        place = columns + 16 * (owner - 1)
        valid = (place >= 0) & (place < 32)
        half = place % 2
        inner = (place // 16) * 8 + (place % 16) // 2
        even = jnp.where(valid, half * 16 + inner, -1)
        odd = jnp.where(valid, 32 + (1 - half) * 16 + inner, -1)
        spot = lax.broadcasted_iota(jnp.int32, (16, 128), 1) % 64
        for kk in range(14):
            hit = even[:, 2 * kk : 2 * kk + 1] == spot
            if 2 * kk + 1 < 27:
                hit = hit | (odd[:, 2 * kk + 1 : 2 * kk + 2] == spot)
            target[kk * 16 : (kk + 1) * 16, :] = jnp.where(hit, 1.0, 0.0).astype(BF16)

    def start_sends(ex, relations, rows):
        copies = []
        for relation in relations:
            slot = QUAD.index(relation)
            copy = pltpu.make_async_remote_copy(
                src_ref=send_buf.at[ex, 0:rows],
                dst_ref=recv_buf.at[ex, slot, 0:rows],
                send_sem=send_sem.at[ex, slot],
                recv_sem=recv_sem.at[ex, slot],
                device_id=peer(relation),
                device_id_type=MESH,
            )
            copy.start()
            copies.append(copy)
        return copies

    started = []

    def own(value):
        return jnp.where(mine, value, 0.0)

    def send(ex, low, high, relations, rows=8):
        send_buf[ex, 0:8] = low
        if high is not None:
            send_buf[ex, 8:16] = high
        copies = start_sends(ex, relations, rows)
        started.extend(copies)
        return copies

    def total(ex, relations, base, rows):
        value = send_buf[ex, base : base + rows]
        for relation in relations:
            value = value + recv_buf[ex, QUAD.index(relation), base : base + rows]
        if rows < 8:
            value = jnp.concatenate([value, jnp.zeros((8 - rows, 128), F32)], axis=0)
        return value

    def restrict_part(y, group, rows):
        cut = slice(group * rows, (group + 1) * rows)
        hi1, lo1 = pieces(y * mask_ref[0, :, cut])
        hi3, lo3 = pieces(y * mask_ref[1, :, cut])
        return mm(jnp.concatenate([hi1, lo1, hi3, lo3], axis=0), wr_ref[cut])

    def restrict_end(out):
        s1 = out[0:8, 0:128] + out[8:16, 0:128]
        s3 = out[16:24, 128:256] + out[24:32, 128:256]
        return s1 + pltpu.roll(s1, 64, 1), s3 + pltpu.roll(s3, 64, 1)

    def restrict(y):
        return restrict_end(restrict_part(y, 0, 1024))

    def prolong(v, level):
        v0 = jnp.where(left, v, 0.0)
        both = jnp.concatenate([v0, v - v0], axis=0)
        hi, lo = pieces(both)
        lhs = jnp.concatenate(
            [
                jnp.concatenate([hi, hi], axis=1),
                jnp.concatenate([lo, jnp.zeros_like(lo)], axis=1),
            ],
            axis=0,
        )
        tiles = [[], []]
        for quarter in range(4):
            prod = mm(lhs, wp_ref[level, :, quarter * 256 : (quarter + 1) * 256])
            prod = prod[0:16] + prod[16:32]
            for dd in range(2):
                for part in range(2):
                    jj = 2 * quarter + part
                    tile = prod[dd * 8 : dd * 8 + 8, part * 128 : (part + 1) * 128]
                    tile = tile * mask_ref[level, :, jj * 128 : (jj + 1) * 128]
                    tile = tile + pltpu.roll(tile, 4, 0)
                    tile = tile + pltpu.roll(tile, 2, 0)
                    tile = tile + pltpu.roll(tile, 1, 0)
                    tiles[dd].append(tile)
        return tiles

    def rows_of(tiles):
        value = tiles[0]
        for jj in range(1, 8):
            value = jnp.where(row == jj, tiles[jj], value)
        return value

    def own_rows(tiles):
        return jnp.where(d == 0, rows_of(tiles[0]), rows_of(tiles[1]))

    def apply(v, level, shifted=True):
        tiles = prolong(v, level)
        u = jnp.concatenate([rows_of(tiles[0]), rows_of(tiles[1])], axis=0)
        turned = pltpu.roll(u, 64, 1)
        left16 = jnp.concatenate([left, left], axis=0)
        spread = jnp.concatenate(
            [
                jnp.where(left16, u, 0.0),
                jnp.where(left16, turned, 0.0),
                jnp.where(left16, 0.0, u),
                jnp.where(left16, 0.0, turned),
            ],
            axis=0,
        )
        hi, lo = pieces(spread)
        rhs = jnp.concatenate([hi, lo], axis=0)
        ug_ref[...] = mm(hot_ref[...], rhs)

        def blocks(numbers, a_ref, u_ref, r_ref, first):
            out = None
            for i in numbers:
                base = (i - first) * 64
                acc = jnp.zeros((8, 8, 128), F32)
                for kk in range(13):
                    u = jnp.broadcast_to(u_ref[kk * 16 + i : kk * 16 + i + 1, :], (8, 128))
                    block = a_ref[base : base + 64, kk * 128 : (kk + 1) * 128]
                    acc = acc + block.reshape(8, 8, 128) * u[None]
                u = jnp.broadcast_to(u_ref[13 * 16 + i : 13 * 16 + i + 1, :], (8, 128))
                tail = a_ref[base : base + 64, 1664:1728].reshape(8, 8, 64) * u[None, :, 0:64]
                acc = acc + jnp.concatenate([tail, jnp.zeros((8, 8, 64), F32)], axis=2)
                y = jnp.sum(acc.reshape(64, 128), axis=1, keepdims=True)
                part = jnp.sum((r_ref[base : base + 64, :] * y).reshape(8, 8, 128), axis=0)
                part = part + pltpu.roll(part, 4, 0)
                part = part + pltpu.roll(part, 2, 0)
                part = (part + pltpu.roll(part, 1, 0)) * pick_ref[i]
                out = part if out is None else out + part
            return out

        if shifted:
            out = blocks(range(16 - SHIFT), a_buf, ug_ref, rt_ref, 0)
            last = range(16 - SHIFT, 16)

            def both_ends():
                ugx_ref[...] = mm(hotx_ref[...], rhs)
                return (
                    blocks(last, a_buf, ug_ref, rt_ref, 0),
                    blocks(last, ax_buf, ugx_ref, rtx_ref, 16 - SHIFT),
                )

            def neither():
                return jnp.zeros((8, 128), F32), jnp.zeros((8, 128), F32)

            more, other = lax.cond(d == 1, both_ends, neither)
            out = out + more
        else:
            out = blocks(range(16), a_buf, ug_ref, rt_ref, 0)
            other = jnp.zeros((8, 128), F32)
        turned = pltpu.roll(out, 64, 1)
        other_turned = pltpu.roll(other, 64, 1)
        w = jnp.where(mine, jnp.where(left, out, turned), jnp.where(left, other, other_turned))
        w3 = jnp.where(mine, jnp.where(left, turned, out), jnp.where(left, other_turned, other))
        return w, w3

    r1_copy.wait()
    own_r1 = r1_buf[pl.ds(pl.multiple_of(d * 64, 64), 64), :]
    hi, lo = pieces(own_r1.T)
    wr_ref[:, 0:64] = hi
    wr_ref[:, 64:128] = lo

    pl.semaphore_wait(barrier, len(QUAD))

    def swap_copy(buf, index):
        ref = buf.at[pl.ds(d * 64, 64)]
        return pltpu.make_async_remote_copy(
            src_ref=ref,
            dst_ref=ref,
            send_sem=rx_send.at[index],
            recv_sem=rx_recv.at[index],
            device_id=(g, 1 - d),
            device_id_type=MESH,
        )

    swap1 = swap_copy(r1_buf, 0)
    swap1.start()
    y0 = jnp.broadcast_to(res_ref[...], (8, 1024))
    hi, lo = pieces(y0 * mask_ref[0])
    w = mm(jnp.concatenate([hi, lo], axis=0), wr_ref[:, 0:128])
    w = w[0:8] + w[8:16]
    w = w + pltpu.roll(w, 64, 1)
    copies = send(0, own(w), None, PAIR)

    for copy in inputs[3:5]:
        copy.wait()
    cols_copy = pltpu.make_async_remote_copy(
        src_ref=cols_ref,
        dst_ref=colsx_ref,
        send_sem=shift_send.at[0],
        recv_sem=shift_recv.at[0],
        device_id=(g, 1 - d),
        device_id_type=MESH,
    )
    cols_copy.start()

    a_copy = pltpu.make_async_remote_copy(
        src_ref=a_hbm.at[pl.ds(64 * (16 - SHIFT), 64 * SHIFT)],
        dst_ref=ax_buf,
        send_sem=shift_send.at[1],
        recv_sem=shift_recv.at[1],
        device_id=(g, 1 - d),
        device_id_type=MESH,
    )

    @pl.when(d == 0)
    def _():
        a_copy.start()

    for m in range(8):
        r2_blk[m] = r2_ref[:, m * 64 : (m + 1) * 64]

    for jj in range(8):
        parts = []
        for half_at in range(2):
            j = 2 * jj + half_at
            parts.append(
                jnp.dot(
                    r2_blk[aggs[j]],
                    own_r1[:, j * 64 : (j + 1) * 64],
                    preferred_element_type=F32,
                    precision=lax.Precision.HIGHEST,
                )
            )
        r31_buf[pl.ds(pl.multiple_of(d * 64, 64), 64), jj * 128 : (jj + 1) * 128] = jnp.concatenate(
            parts, axis=1
        )
    own_r31 = r31_buf[pl.ds(pl.multiple_of(d * 64, 64), 64), :]
    swap3 = swap_copy(r31_buf, 1)
    swap3.start()
    hi, lo = pieces(own_r31.T)
    rt_ref[:, 64:128] = own_r31.T
    wr_ref[:, 128:192] = hi
    wr_ref[:, 192:256] = lo
    unused, coarse = restrict(y0)
    coarse = own(coarse)

    swap1.wait()
    hi, lo = pieces(r1_buf[...])
    wp_ref[0, 0:128] = hi
    wp_ref[0, 128:256] = lo

    for j in range(16):
        pick_ref[j] = jnp.where(jnp.where(left, aggs[j], agg2_ref[aggs[j]] // 2) == row, 1.0, 0.0)

    rt_ref[:, 0:64] = own_r1.T
    build_hot(cols_ref[...], d, hot_ref)
    cols_copy.wait()
    build_hot(colsx_ref[...], 1 - d, hotx_ref)
    rtx_ref[:, 0:64] = r1_buf[pl.ds(pl.multiple_of((1 - d) * 64, 64), 64), 64 * (16 - SHIFT) :].T
    swap3.wait()
    rtx_ref[:, 64:128] = r31_buf[pl.ds(pl.multiple_of((1 - d) * 64, 64), 64), 64 * (16 - SHIFT) :].T
    for copy in a_copies:
        copy.wait()

    spread_ratio = CENTER_VALUE / HALF_WIDTH

    def wait_all(copies):
        for copy in copies:
            copy.wait_recv()

    def pair_total(ex, copies):
        wait_all(copies)
        return total(ex, PAIR, 0, 8)

    def quad_total(ex, copies):
        wait_all(copies)
        return total(ex, QUAD, 0, 4)

    rest = pair_total(0, copies)
    start = jnp.zeros((8, 128), F32)
    direction = rest / CENTER_VALUE
    ratio = 1.0 / spread_ratio
    for sweep in range(S2):
        ex = 1 + sweep
        start = start + direction
        if sweep == SHIFT_FROM:

            @pl.when(d == 1)
            def _():
                a_copy.wait_recv()

        w, w3 = apply(direction, 0, sweep >= SHIFT_FROM)
        coarse = coarse - w3
        if sweep == S2 - 1:
            copies = send(ex, w, coarse, QUAD, 12)
            wait_all(copies)
            rest = rest - total(ex, PAIR, 0, 8)
            rhs3 = total(ex, QUAD, 8, 4)
        else:
            copies = send(ex, w, None, PAIR)
            if sweep == 0:
                hi, lo = pieces(r31_buf[...])
                wp_ref[1, 0:128] = hi
                wp_ref[1, 128:256] = lo
            rest = rest - pair_total(ex, copies)
            ratio_next = 1.0 / (2.0 * spread_ratio - ratio)
            direction = ratio_next * ratio * direction + 2.0 * ratio_next / HALF_WIDTH * rest
            ratio = ratio_next

    rest3 = rhs3
    coarse_sol = jnp.zeros((8, 128), F32)
    direction = rest3 / CENTER_VALUE
    ratio = 1.0 / spread_ratio
    for sweep in range(S3):
        coarse_sol = coarse_sol + direction
        if sweep < S3 - 1:
            ex = 1 + S2 + sweep
            unused, w3 = apply(direction, 1)
            copies = send(ex, w3, None, QUAD, 4)
            rest3 = rest3 - quad_total(ex, copies)
            ratio_next = 1.0 / (2.0 * spread_ratio - ratio)
            direction = ratio_next * ratio * direction + 2.0 * ratio_next / HALF_WIDTH * rest3
            ratio = ratio_next

    ex = S2 + S3
    w, unused = apply(coarse_sol, 1)
    copies = send(ex, w, None, PAIR)
    fine_coarse = own_rows(prolong(coarse_sol, 1))
    rest = rest - pair_total(ex, copies)
    direction = rest / CENTER_VALUE
    ratio = 1.0 / spread_ratio
    for sweep in range(S2):
        start = start + direction
        if sweep < S2 - 1:
            ex = S2 + S3 + 1 + sweep
            w, unused = apply(direction, 0)
            copies = send(ex, w, None, PAIR)
            rest = rest - pair_total(ex, copies)
            ratio_next = 1.0 / (2.0 * spread_ratio - ratio)
            direction = ratio_next * ratio * direction + 2.0 * ratio_next / HALF_WIDTH * rest
            ratio = ratio_next

    out_ref[...] = own_rows(prolong(start, 0)) + fine_coarse

    for copy in started:
        copy.wait_send()

    @pl.when(d == 0)
    def _():
        a_copy.wait_send()


def body(residual, op_blocks, block_cols, restrict_one, restrict_two, agg_one, agg_two):
    vmem = pl.BlockSpec(memory_space=pltpu.VMEM)
    hbm = pl.BlockSpec(memory_space=pltpu.HBM)
    out = pl.pallas_call(
        kernel,
        out_shape=jax.ShapeDtypeStruct((8, 128), F32),
        in_specs=[hbm] * 7,
        out_specs=vmem,
        scratch_shapes=[
            pltpu.SMEM((16,), jnp.int32),
            pltpu.SMEM((8,), jnp.int32),
            pltpu.VMEM((1, 1024), F32),
            pltpu.VMEM((16, 27), jnp.int32),
            pltpu.VMEM((64, 512), F32),
            pltpu.VMEM((1024, 1728), F32),
            pltpu.VMEM((128, 1024), F32),
            pltpu.VMEM((128, 1024), F32),
            pltpu.VMEM((8, 64, 64), F32),
            pltpu.VMEM((2, 256, 1024), BF16),
            pltpu.VMEM((1024, 256), BF16),
            pltpu.VMEM((2, 8, 1024), F32),
            pltpu.VMEM((224, 128), BF16),
            pltpu.VMEM((224, 128), F32),
            pltpu.VMEM((64 * SHIFT, 1728), F32),
            pltpu.VMEM((16, 27), jnp.int32),
            pltpu.VMEM((224, 128), BF16),
            pltpu.VMEM((224, 128), F32),
            pltpu.VMEM((64 * SHIFT, 128), F32),
            pltpu.SemaphoreType.DMA((2,)),
            pltpu.SemaphoreType.DMA((2,)),
            pltpu.VMEM((1024, 128), F32),
            pltpu.VMEM((16, 8, 128), F32),
            pltpu.VMEM((N_EX, 16, 128), F32),
            pltpu.VMEM((N_EX, len(QUAD), 16, 128), F32),
            pltpu.SemaphoreType.DMA((A_CHUNKS,)),
            pltpu.SemaphoreType.DMA,
            pltpu.SemaphoreType.DMA((5,)),
            pltpu.SemaphoreType.DMA((2,)),
            pltpu.SemaphoreType.DMA((2,)),
            pltpu.SemaphoreType.DMA((N_EX, len(QUAD))),
            pltpu.SemaphoreType.DMA((N_EX, len(QUAD))),
        ],
        compiler_params=pltpu.CompilerParams(
            collective_id=0, has_side_effects=True, vmem_limit_bytes=48 * 1024 * 1024
        ),
        cost_estimate=pl.CostEstimate(
            flops=40_000_000, bytes_accessed=7_500_000, transcendentals=0
        ),
    )(
        *(
            pltpu.with_memory_space_constraint(value, pltpu.HBM)
            for value in (
                agg_one,
                agg_two,
                residual,
                block_cols[0],
                restrict_two,
                restrict_one[0],
                op_blocks.reshape(1024, 1728),
            )
        )
    )
    return out.reshape(1, 1024)


def solution(mesh):
    placed = (
        P("grp", "dom"),
        P("grp", "dom", None, None),
        P("grp", "dom", None),
        P("grp", None, "dom"),
        P(None, "dom"),
        P(),
        P(),
    )
    return jax.shard_map(
        body, mesh=mesh, in_specs=placed, out_specs=P("grp", "dom"), check_vma=False
    )
```
